128 devices in a mesh: grp: 16 (over y_lo, x, core), tile: 8 (over y_hi, z).
Axes of the slice: x: 4, y: 4 (y_hi: 2, y_lo: 2; y = y_hi * 2 + y_lo), z: 4, core: 2. Of those that a mesh axis runs over, the one named last changes fastest.
Arguments:
- coeff: bfloat16 [64, 256, 4096], P('grp', None, 'tile'), may hold values from -0.09375 to 0.09375
- energy: float32 [64, 4096], P('grp', 'tile'), may hold values from 1 to 3
- ranks: int32 [64, 64], replicated, may hold values from 32 to 256, as said below
- assign: int32 [4096], P(('grp', 'tile')), may hold values from 0 to 4095, each once
- screen: bfloat16 [4096, 256, 256], P(('grp', 'tile')), may hold values from -0.375 to 0.375
- initial: float32 [64, 8, 4096], P('grp', None, 'tile'), may hold values from -6 to 6
Outputs:
- rayleigh: float32 [2, 8, 8], replicated
- basis: float32 [64, 8, 4096], P('grp', None, 'tile')
- residual: float32 [64, 8, 4096], P('grp', None, 'tile')
The draws below stay inside these ranges and needn't reach their ends.
Inputs may be any that keep to these rules, and one draw needn't show every extreme that they name: ranks is symmetric and its diagonal equals 256. `assign`: every pair index appears exactly once.
All inputs are finite; a program needn't handle non-finite values.
Results may differ from the reference program's by a relative error of at most 0.0075.
Values may be sent and summed in bfloat16 or wider, within the bound.
A program may use at most 64 MiB of HBM per device.

```python
import jax
import jax.numpy as jnp
from jax import lax

P_SIZE = 4096
RMAX = 256
NV = 8
ITERS = 2
K = 64


def draw_ranks(key, part):
    base = jax.random.randint(key, (K, K), RMAX // 8, RMAX + 1)
    upper = jnp.triu(base, 1)
    ident = jnp.eye(K, dtype=jnp.int32)
    return (upper + upper.T + ident * RMAX).astype(jnp.int32)


def level_of(rng, extent, split, smallest, high):
    factor_of = 1.0
    for dim, parts in split:
        heights = jax.random.uniform(jax.random.fold_in(jax.random.fold_in(rng, 6), dim), (parts,), jnp.float32, smallest / len(split), high / len(split))
        factor_of = factor_of * jnp.repeat(jnp.exp(heights), extent[dim] // parts).reshape((-1,) + (1,) * (len(extent) - 1 - dim))
    return factor_of


def gaussian(stream_key, extent, scale, bound, split=(), held_as=jnp.bfloat16):
    gain = level_of(stream_key, extent, split, -0.22, 0.18) if split else 1.0
    values = jax.random.normal(stream_key, extent, jnp.float32) * scale * gain
    return jnp.minimum(jnp.maximum(values, -bound), bound).astype(held_as)


def setup_inputs(seed: int = 0) -> dict:
    seeds = jax.random.split(jax.random.key(seed), 7)
    coeff = gaussian(seeds[0], (K, RMAX, P_SIZE), P_SIZE ** -0.5, 0.09375, ((0, 16), (2, 8)))
    energy = jnp.clip(1.0 + 2.0 * jax.random.uniform(seeds[1], (K, P_SIZE), jnp.float32) ** level_of(seeds[1], (K, P_SIZE), ((0, 16), (1, 8)), -0.2, 0.2), 1.0, 3.0)
    ranks = draw_ranks(jax.random.fold_in(seeds[6], 71), 0)
    assign = jax.random.permutation(seeds[3], K * K).astype(jnp.int32)
    screen = gaussian(seeds[4], (K * K, RMAX, RMAX), RMAX ** -0.5, 0.375, ((0, 128),))
    initial = gaussian(seeds[5], (K, NV, P_SIZE), 1.0, 6.0, ((0, 16), (2, 8)), jnp.float32)
    return dict(coeff=coeff, energy=energy, ranks=ranks, assign=assign, screen=screen, initial=initial)


def inner_sum(left, right):
    return jnp.einsum('knp,kmp->nm', left, right, precision=lax.Precision.HIGHEST)

def combine_rows(weights, block):
    return jnp.einsum('mn,kmp->knp', weights, block, precision=lax.Precision.HIGHEST)

def orthonormal(block, count):
    gram = inner_sum(block, block) / count
    lower = jnp.linalg.cholesky(gram)
    inverse = lax.linalg.triangular_solve(lower, jnp.eye(NV, dtype=jnp.float32), left_side=True, lower=True)
    return combine_rows(inverse.T, block)

def apply_kernel(block, coeff, energy, ranks, assign, screen):
    block_b = block.astype(jnp.bfloat16)

    def project_one(pair):
        return jnp.dot(pair[1].astype(jnp.float32), pair[0].T.astype(jnp.float32), preferred_element_type=jnp.float32)
    dens = lax.map(project_one, (coeff, block_b))
    dens_b = dens.astype(jnp.bfloat16)
    task_row = (assign // K).astype(jnp.int32)
    task_col = (assign % K).astype(jnp.int32)
    task_rank = ranks[task_row, task_col]
    levels = jnp.arange(RMAX, dtype=jnp.int32)

    def task_one(item):
        blocks, column, rank_now = item
        keep = (levels < rank_now).astype(jnp.float32)
        masked = dens_b[column] * keep.astype(jnp.bfloat16)[None, :]
        result = jnp.dot(masked.astype(jnp.float32), blocks.T.astype(jnp.float32), preferred_element_type=jnp.float32)
        return result * keep[None, :]
    terms = lax.map(task_one, (screen, task_col, task_rank))
    rows = jax.ops.segment_sum(terms, task_row, num_segments=K)
    rows_b = rows.astype(jnp.bfloat16)

    def expand_one(pair):
        return jnp.dot(pair[1].astype(jnp.float32), pair[0].astype(jnp.float32), preferred_element_type=jnp.float32)
    coupled = lax.map(expand_one, (coeff, rows_b))
    return energy[:, None, :] * block + coupled

def reference(coeff, energy, ranks, assign, screen, initial):
    count = K * P_SIZE
    basis = orthonormal(initial, count)
    collected = []
    residual = initial
    for step in range(ITERS):
        sigma = apply_kernel(basis, coeff, energy, ranks, assign, screen)
        projected = inner_sum(basis, sigma) / count
        collected.append(projected)
        residual = sigma - combine_rows(projected, basis)
        precond = residual / energy[:, None, :]
        correlation = inner_sum(basis, precond) / count
        direction = precond - combine_rows(correlation, basis)
        basis = orthonormal(direction, count)
    return (jnp.stack(collected), basis, residual)
```

```python
import functools

import jax
import jax.numpy as jnp
from jax import lax
from jax.experimental import pallas as pl
from jax.experimental.pallas import tpu as pltpu
from jax.sharding import PartitionSpec as P

ITERS = 2
NV = 8
GRP, TILE, CHIPS, CORES = 16, 8, 8, 2
LK = 4
ROWS = LK * NV
ALL = GRP * ROWS
LEV = 256
TASKS = 32
SPAN = 128
F32, BF16 = jnp.float32, jnp.bfloat16
HIGHEST = lax.Precision.HIGHEST
MESH = pl.DeviceIdType.MESH
CHIP_STEPS = ((1, 2), (0, 2), (1, 1), (1, 3), (0, 1), (0, 3), (1, 0))
TILE_STEPS = ((1, 2), (1, 1), (1, 3), (1, 0), (0, 2), (0, 1), (0, 3))


def dot(a, b, nt=False, precision=None):
    return lax.dot_general(
        a, b, (((1,), (1 if nt else 0,)), ((), ())),
        precision=precision, preferred_element_type=F32,
    )


def split(a):
    high = a.astype(BF16)
    return high, (a - high.astype(F32)).astype(BF16)


def iota(shape, dim):
    return lax.broadcasted_iota(jnp.int32, shape, dim)


def block_mask(rows, cols):
    return (iota((rows, cols), 0) // NV) == (iota((rows, cols), 1) // NV)


def fold(part):
    for step in (8, 16, 32, 64):
        part = part + pltpu.roll(part, step, 1)
    return part


def sum_groups(a):
    total = a[0:NV]
    for i in range(1, a.shape[0] // NV):
        total = total + a[i * NV:(i + 1) * NV]
    return total


def spread(small, mask):
    return jnp.where(mask, jnp.concatenate([small] * (SPAN // NV), axis=0), 0.0)


def inverse_factor(gram):
    sub, lane = iota((NV, SPAN), 0), iota((NV, SPAN), 1) % NV
    right = (sub == lane).astype(F32)
    pivots = jnp.ones((NV, SPAN), F32)
    for j in range(NV):
        row, other = gram[j:j + 1, :], right[j:j + 1, :]
        pivot = jnp.broadcast_to(row[:, j:j + 1], (NV, SPAN))
        pivots = jnp.where(sub == j, pivot, pivots)
        factor = jnp.broadcast_to(gram[:, j:j + 1], (NV, SPAN)) / pivot
        factor = jnp.where(sub > j, factor, 0.0)
        gram = gram - factor * row
        right = right - factor * other
    return right * lax.rsqrt(pivots)


def body(
    count, assign_ref, ranks_ref, coeff_hbm, screen_hbm, energy_ref, x_ref,
    ray_ref, basis_ref, res_ref,
    coeff, screen, d1, d2, dens, term, part, e8, pick, keep,
    r1s, r1, a1s, a1, r2s, r2, a2, r3, a3, f1, f2,
    load_sem, send, recv,
):
    g, t = lax.axis_index("grp"), lax.axis_index("tile")
    core, chip = lax.rem(g, CORES), lax.div(g, CORES)
    y_lo, x = lax.div(chip, 4), lax.rem(chip, 4)
    y_hi, z = lax.div(t, 4), lax.rem(t, 4)
    sibling = (chip * CORES + (1 - core), t)
    chip_ids = [lax.rem(y_lo + a, 2) * 4 + lax.rem(x + b, 4) for a, b in CHIP_STEPS]
    chips = [(c * CORES + core, t) for c in chip_ids]
    tiles = [(g, lax.rem(y_hi + a, 2) * 4 + lax.rem(z + b, 4)) for a, b in TILE_STEPS]

    half_rows = ALL // 2
    barrier = pltpu.get_barrier_semaphore()
    peers = [sibling, *chips, *tiles]
    for peer in peers:
        pl.semaphore_signal(barrier, inc=1, device_id=peer, device_id_type=MESH)
    load_coeff = pltpu.make_async_copy(coeff_hbm, coeff, load_sem.at[0])
    load_screen = pltpu.make_async_copy(screen_hbm, screen, load_sem.at[1])
    load_coeff.start()
    load_screen.start()

    used = []

    def push(src, dst, index, device):
        pltpu.make_async_remote_copy(
            src_ref=src, dst_ref=dst, send_sem=send.at[index], recv_sem=recv.at[index],
            device_id=device, device_id_type=MESH,
        ).start()

    def await_bytes(ref, sems, index):
        pltpu.make_async_copy(ref, ref, sems.at[index]).wait()

    def gather(buf, mine, devices, index):
        for device in devices:
            push(buf.at[mine], buf.at[mine], index, device)
        await_bytes(buf.at[pl.ds(0, len(devices))], recv, index)
        used.append((buf.at[pl.ds(0, len(devices))], index))

    mask = block_mask(SPAN, SPAN)
    mask_gram = ((iota((2 * ROWS, 2 * ROWS), 0) % ROWS) // NV) == (
        (iota((2 * ROWS, 2 * ROWS), 1) % ROWS) // NV
    )
    section = iota((NV, SPAN), 1) // ROWS

    def grams(left, right):
        full = jnp.where(mask_gram, dot(left, right, nt=True, precision=HIGHEST), 0.0)
        return jnp.concatenate([sum_groups(full[:ROWS]), sum_groups(full[ROWS:])], axis=1)

    def project(block):
        high, low = split(block)
        out = []
        for k in range(LK):
            rows = slice(k * NV, (k + 1) * NV)
            both = jnp.concatenate([block[rows], low[rows].astype(F32)], axis=0).astype(BF16)
            got = dot(both, coeff[k], nt=True)
            out.append(got[:NV] + got[NV:])
        return jnp.concatenate(out, axis=0)

    def section_of(total, which):
        return fold(jnp.where(section == which, total, 0.0)) * (1.0 / count)

    energy = jnp.concatenate(
        [jnp.broadcast_to(energy_ref[k:k + 1, :], (NV, energy_ref.shape[1])) for k in range(LK)],
        axis=0,
    )
    block = x_ref[...]
    scaled = energy * block
    zeros = jnp.zeros_like(block)
    load_coeff.wait()
    payload = project(block)
    sums = grams(jnp.concatenate([block, scaled], 0), jnp.concatenate([zeros, block], 0))

    def place(k):
        return ((k >> 2) & 1) * half_rows + (k >> 3) * ROWS + (k & 3) * NV

    lane_task = iota((1, half_rows), 1) // NV
    target = jnp.zeros((1, half_rows), jnp.int32)
    pairs = []
    for i in range(TASKS):
        pair = assign_ref[i]
        target = jnp.where(lane_task == i, place(pair >> 6), target)
        pairs.append(jnp.full((NV, SPAN), pair, jnp.int32))
    target = target + iota((1, half_rows), 1) % NV
    e8[...] = (iota((ALL, half_rows), 0) == target).astype(F32).astype(BF16)
    pairs = jnp.concatenate(pairs, axis=0)
    task_row, task_col = pairs >> 6, pairs & 63
    lane = iota((half_rows, SPAN), 1)
    source_row = place(task_col) + iota((half_rows, SPAN), 0) % NV
    for j in range(ALL // SPAN):
        pick[:, j * SPAN:(j + 1) * SPAN] = (lane + j * SPAN == source_row).astype(F32).astype(BF16)
    chosen = dot((lane[:, :GRP * LK] == task_row[:, :GRP * LK]).astype(F32).astype(BF16),
                 ranks_ref[...].astype(F32).astype(BF16))
    chosen = jnp.where(lane[:, :GRP * LK] == task_col[:, :GRP * LK], chosen, 0.0)
    rank = jnp.sum(chosen, axis=1, keepdims=True)
    keep[...] = (iota((half_rows, LEV), 1).astype(F32) < rank).astype(F32)

    pl.semaphore_wait(barrier, len(peers))

    basis = None
    own_energy = None
    for step in range(ITERS):
        d1[step, t, 0:ROWS, :] = payload
        d1[step, t, ROWS:, :] = jnp.concatenate([sums, jnp.zeros_like(sums)], axis=1)
        gather(d1.at[step], t, tiles, 10 * step + 0)
        total = d1[step, 0]
        for i in range(1, TILE):
            total = total + d1[step, i]
        d2[step, core, chip] = total
        gather(d2.at[step, core], chip, chips, 10 * step + 1)
        push(d2.at[step, core], d2.at[step, core], 10 * step + 2, sibling)
        await_bytes(d2.at[step, 0], recv, 10 * step + 2)
        used.append((d2.at[step, 0], 10 * step + 2))

        total = jnp.zeros((NV, SPAN), F32)
        for i in range(CHIPS):
            for c in range(CORES):
                total = total + d2[step, c, i, ROWS:, 0:SPAN]
        pv, pp, rv, rp = [section_of(total, i) for i in range(4)]
        pv_spread = spread(pv, mask)
        if step == 0:
            gram = pp
        else:
            gram = pp - dot(pv, pv_spread, nt=True, precision=HIGHEST)
        inverse = inverse_factor(gram)
        inverse_spread = spread(inverse, mask)
        inv_high, inv_low = split(inverse_spread)
        pv_high, pv_low = split(pv_spread)

        def apply(high, low, rows):
            rows_high, rows_low = split(rows)
            return (
                dot(jnp.concatenate([high, high], axis=1), jnp.concatenate([rows_high, rows_low], axis=0))
                + dot(low, rows_high)
            )

        for j in range(ALL // SPAN):
            raw = jnp.concatenate(
                [d2[step, j // 2, (j % 2) * 4 + i, 0:ROWS, :] for i in range(4)], axis=0
            )
            if step:
                raw = raw - apply(pv_high, pv_low, dens[step - 1, j * SPAN:(j + 1) * SPAN, :])
            dens[step, j * SPAN:(j + 1) * SPAN, :] = apply(inv_high, inv_low, raw)

        if step:
            block = block - dot(pv_spread[:ROWS, :ROWS], basis, precision=HIGHEST)
            crossed = dot(rv, pv_spread, nt=True, precision=HIGHEST)
            crossed_t = dot(pv, spread(rv, mask), nt=True, precision=HIGHEST)
            inner = dot(pv, spread(own_energy, mask), precision=HIGHEST)
            rp = rp - crossed - crossed_t + dot(inner, pv_spread, nt=True, precision=HIGHEST)
        basis = dot(inverse_spread[:ROWS, :ROWS], block, precision=HIGHEST)
        half = dot(inverse, spread(rp, mask), precision=HIGHEST)
        own_energy = dot(half, inverse_spread, nt=True, precision=HIGHEST)

        if step == 0:
            load_screen.wait()
        chosen = dot(pick[...], dens[step].astype(BF16)) * keep[...]
        for i in range(TASKS):
            rows = slice(i * NV, (i + 1) * NV)
            term[rows, :] = dot(chosen[rows].astype(BF16), screen[i], nt=True)
        term_high, term_low = split(term[...] * keep[...])
        part[...] = dot(e8[...], term_high) + dot(e8[...], term_low)
        coupled = jnp.zeros((SPAN, SPAN), F32)
        for j in range(ALL // SPAN):
            rows = slice(j * SPAN, (j + 1) * SPAN)
            coupled = coupled + dot(part[rows, :].astype(BF16), dens[step, rows, :].astype(BF16), nt=True)
        coupled = sum_groups(jnp.where(mask, coupled, 0.0))

        theirs = pl.ds(pl.multiple_of((1 - core) * half_rows, half_rows), half_rows)
        r1s[step] = part[theirs, :].astype(BF16)
        a1s[step] = coupled
        push(r1s.at[step], r1.at[step], 10 * step + 3, sibling)
        push(a1s.at[step], a1.at[step], 10 * step + 4, sibling)
        mine = part[pl.ds(pl.multiple_of(core * half_rows, half_rows), half_rows), :]
        await_bytes(r1.at[step], recv, 10 * step + 3)
        await_bytes(a1.at[step], recv, 10 * step + 4)
        used.append((r1.at[step], 10 * step + 3))
        used.append((a1.at[step], 10 * step + 4))
        summed = (mine + r1[step].astype(F32)).astype(BF16)
        for i in range(CHIPS):
            r2s[step, i] = summed[i * ROWS:(i + 1) * ROWS]
        a2[step, chip] = coupled + a1[step]
        for c, device in zip(chip_ids, chips):
            push(r2s.at[step, c], r2.at[step, chip], 10 * step + 5, device)
        gather_index = 10 * step + 6
        r2[step, chip] = r2s[step, chip]
        gather(a2.at[step], chip, chips, gather_index)
        await_bytes(r2.at[step, pl.ds(0, CHIPS - 1)], recv, 10 * step + 5)
        used.append((r2.at[step, pl.ds(0, CHIPS - 1)], 10 * step + 5))
        rows_sum = r2[step, 0].astype(F32)
        a_sum = a2[step, 0]
        for i in range(1, CHIPS):
            rows_sum = rows_sum + r2[step, i].astype(F32)
            a_sum = a_sum + a2[step, i]
        r3[step, t] = rows_sum.astype(BF16)
        a3[step, t] = a_sum
        for device in tiles:
            push(r3.at[step, t], r3.at[step, t], 10 * step + 7, device)
        gather(a3.at[step], t, tiles, 10 * step + 8)
        await_bytes(r3.at[step, pl.ds(0, TILE - 1)], recv, 10 * step + 7)
        used.append((r3.at[step, pl.ds(0, TILE - 1)], 10 * step + 7))
        rows_sum = r3[step, 0].astype(F32)
        a_sum = a3[step, 0]
        for i in range(1, TILE):
            rows_sum = rows_sum + r3[step, i].astype(F32)
            a_sum = a_sum + a3[step, i]

        ray_t = fold(a_sum) * (1.0 / count) + own_energy
        eye = (iota((NV, SPAN), 0) == iota((NV, SPAN), 1)).astype(F32)
        first = jnp.where(iota((NV, SPAN), 1) < NV, ray_t, 0.0)
        ray_ref[step] = dot(eye, first, nt=True, precision=HIGHEST)
        rows_b = rows_sum.astype(BF16)
        sigma = energy * basis + jnp.concatenate(
            [dot(rows_b[k * NV:(k + 1) * NV], coeff[k]) for k in range(LK)], axis=0
        )
        residual = sigma - dot(spread(ray_t, mask)[:ROWS, :ROWS], basis, precision=HIGHEST)
        block = residual / energy
        sums = grams(
            jnp.concatenate([block, residual], 0), jnp.concatenate([basis, block], 0)
        )
        if step + 1 < ITERS:
            payload = project(block)

    res_ref[...] = residual
    f1[t] = sums
    gather(f1, t, tiles, 10 * ITERS)
    total = f1[0]
    for i in range(1, TILE):
        total = total + f1[i]
    f2[core, chip] = total
    gather(f2.at[core], chip, chips, 10 * ITERS + 1)
    push(f2.at[core], f2.at[core], 10 * ITERS + 2, sibling)
    await_bytes(f2.at[0], recv, 10 * ITERS + 2)
    used.append((f2.at[0], 10 * ITERS + 2))
    total = jnp.zeros((NV, SPAN), F32)
    for i in range(CHIPS):
        for c in range(CORES):
            total = total + f2[c, i]
    pv, pp = section_of(total, 0), section_of(total, 1)
    pv_spread = spread(pv, mask)
    gram = pp - dot(pv, pv_spread, nt=True, precision=HIGHEST)
    inverse_spread = spread(inverse_factor(gram), mask)
    block = block - dot(pv_spread[:ROWS, :ROWS], basis, precision=HIGHEST)
    basis_ref[...] = dot(inverse_spread[:ROWS, :ROWS], block, precision=HIGHEST)

    for ref, index in used:
        await_bytes(ref, send, index)


def per_device(coeff, energy, ranks, assign, screen, initial):
    width = initial.shape[2]
    count = initial.shape[0] * GRP * width * TILE
    vmem = pl.BlockSpec(memory_space=pltpu.VMEM)
    smem = pl.BlockSpec(memory_space=pltpu.SMEM)
    anywhere = pl.BlockSpec(memory_space=pl.ANY)
    phases = 10 * ITERS + 3
    ray, basis, residual = pl.pallas_call(
        functools.partial(body, count),
        out_shape=[
            jax.ShapeDtypeStruct((ITERS, NV, NV), F32),
            jax.ShapeDtypeStruct((ROWS, width), F32),
            jax.ShapeDtypeStruct((ROWS, width), F32),
        ],
        in_specs=[smem, vmem, anywhere, anywhere, vmem, vmem],
        out_specs=[vmem, vmem, vmem],
        scratch_shapes=[
            pltpu.VMEM(coeff.shape, BF16),
            pltpu.VMEM(screen.shape, BF16),
            pltpu.VMEM((ITERS, TILE, ROWS + NV, LEV), F32),
            pltpu.VMEM((ITERS, CORES, CHIPS, ROWS + NV, LEV), F32),
            pltpu.VMEM((ITERS, ALL, LEV), F32),
            pltpu.VMEM((ALL // 2, LEV), F32),
            pltpu.VMEM((ALL, LEV), F32),
            pltpu.VMEM((ALL, ALL // 2), BF16),
            pltpu.VMEM((ALL // 2, ALL), BF16),
            pltpu.VMEM((ALL // 2, LEV), F32),
            pltpu.VMEM((ITERS, ALL // 2, LEV), BF16),
            pltpu.VMEM((ITERS, ALL // 2, LEV), BF16),
            pltpu.VMEM((ITERS, NV, SPAN), F32),
            pltpu.VMEM((ITERS, NV, SPAN), F32),
            pltpu.VMEM((ITERS, CHIPS, ROWS, LEV), BF16),
            pltpu.VMEM((ITERS, CHIPS, ROWS, LEV), BF16),
            pltpu.VMEM((ITERS, CHIPS, NV, SPAN), F32),
            pltpu.VMEM((ITERS, TILE, ROWS, LEV), BF16),
            pltpu.VMEM((ITERS, TILE, NV, SPAN), F32),
            pltpu.VMEM((TILE, NV, SPAN), F32),
            pltpu.VMEM((CORES, CHIPS, NV, SPAN), F32),
            pltpu.SemaphoreType.DMA((2,)),
            pltpu.SemaphoreType.DMA((phases,)),
            pltpu.SemaphoreType.DMA((phases,)),
        ],
        compiler_params=pltpu.CompilerParams(
            collective_id=0, has_side_effects=True, vmem_limit_bytes=48 * 2**20
        ),
        name="davidson",
    )(assign, ranks, coeff, screen, energy, initial.reshape(ROWS, width))
    return ray, basis.reshape(initial.shape), residual.reshape(initial.shape)


def solution(mesh):
    placed = (
        P("grp", None, "tile"),
        P("grp", "tile"),
        P(),
        P(("grp", "tile")),
        P(("grp", "tile"), None, None),
        P("grp", None, "tile"),
    )
    return jax.shard_map(
        per_device,
        mesh=mesh,
        in_specs=placed,
        out_specs=(P(), P("grp", None, "tile"), P("grp", None, "tile")),
        check_vma=False,
    )
```

```python
import functools

import jax
import jax.numpy as jnp
from jax import lax
from jax.experimental import pallas as pl
from jax.experimental.pallas import tpu as pltpu
from jax.sharding import PartitionSpec as P

ITERS = 2
NV = 8
GRP, TILE, CHIPS, CORES = 16, 8, 8, 2
LK = 4
ROWS = LK * NV
ALL = GRP * ROWS
LEV = 256
TASKS = 32
SPAN = 128
F32, BF16 = jnp.float32, jnp.bfloat16
HIGHEST = lax.Precision.HIGHEST
MESH = pl.DeviceIdType.MESH
CHIP_STEPS = ((1, 2), (0, 2), (1, 1), (1, 3), (0, 1), (0, 3), (1, 0))
TILE_STEPS = ((1, 2), (1, 1), (1, 3), (1, 0), (0, 2), (0, 1), (0, 3))


def dot(a, b, nt=False, precision=None):
    return lax.dot_general(
        a, b, (((1,), (1 if nt else 0,)), ((), ())),
        precision=precision, preferred_element_type=F32,
    )


def split(a):
    high = a.astype(BF16)
    return high, (a - high.astype(F32)).astype(BF16)


def iota(shape, dim):
    return lax.broadcasted_iota(jnp.int32, shape, dim)


def block_mask(rows, cols):
    return (iota((rows, cols), 0) // NV) == (iota((rows, cols), 1) // NV)


def fold(part):
    for step in (8, 16, 32, 64):
        part = part + pltpu.roll(part, step, 1)
    return part


def sum_groups(a):
    total = a[0:NV]
    for i in range(1, a.shape[0] // NV):
        total = total + a[i * NV:(i + 1) * NV]
    return total


def spread(small, mask):
    return jnp.where(mask, jnp.concatenate([small] * (SPAN // NV), axis=0), 0.0)


def inverse_factor(gram):
    sub, lane = iota((NV, SPAN), 0), iota((NV, SPAN), 1) % NV
    right = (sub == lane).astype(F32)
    pivots = jnp.ones((NV, SPAN), F32)
    for j in range(NV):
        row, other = gram[j:j + 1, :], right[j:j + 1, :]
        pivot = jnp.broadcast_to(row[:, j:j + 1], (NV, SPAN))
        pivots = jnp.where(sub == j, pivot, pivots)
        factor = jnp.broadcast_to(gram[:, j:j + 1], (NV, SPAN)) / pivot
        factor = jnp.where(sub > j, factor, 0.0)
        gram = gram - factor * row
        right = right - factor * other
    return right * lax.rsqrt(pivots)


def body(
    count, assign_hbm, ranks_hbm, coeff_hbm, screen_hbm, energy_hbm, x_hbm,
    ray_ref, basis_ref, res_ref,
    coeff, screen, d1, d2, dens, term, part, e8, pick, keep,
    r1s, r1, a1s, a1, r2s, r2, a2, r3, a3, f1, f2,
    assign_ref, ranks_ref, energy_ref, x_ref, load_sem, send, recv,
):
    g, t = lax.axis_index("grp"), lax.axis_index("tile")
    core, chip = lax.rem(g, CORES), lax.div(g, CORES)
    y_lo, x = lax.div(chip, 4), lax.rem(chip, 4)
    y_hi, z = lax.div(t, 4), lax.rem(t, 4)
    sibling = (chip * CORES + (1 - core), t)
    chip_ids = [lax.rem(y_lo + a, 2) * 4 + lax.rem(x + b, 4) for a, b in CHIP_STEPS]
    chips = [(c * CORES + core, t) for c in chip_ids]
    tiles = [(g, lax.rem(y_hi + a, 2) * 4 + lax.rem(z + b, 4)) for a, b in TILE_STEPS]

    half_rows = ALL // 2
    barrier = pltpu.get_barrier_semaphore()
    peers = [sibling, *chips, *tiles]
    for peer in peers:
        pl.semaphore_signal(barrier, inc=1, device_id=peer, device_id_type=MESH)
    loads = [
        pltpu.make_async_copy(src, dst, load_sem.at[i])
        for i, (src, dst) in enumerate((
            (x_hbm, x_ref), (coeff_hbm, coeff), (energy_hbm, energy_ref),
            (assign_hbm, assign_ref), (ranks_hbm, ranks_ref), (screen_hbm, screen),
        ))
    ]
    for load in loads:
        load.start()

    used = []

    def push(src, dst, index, device):
        pltpu.make_async_remote_copy(
            src_ref=src, dst_ref=dst, send_sem=send.at[index], recv_sem=recv.at[index],
            device_id=device, device_id_type=MESH,
        ).start()

    def await_bytes(ref, sems, index):
        pltpu.make_async_copy(ref, ref, sems.at[index]).wait()

    def gather(buf, mine, devices, index):
        for device in devices:
            push(buf.at[mine], buf.at[mine], index, device)
        await_bytes(buf.at[pl.ds(0, len(devices))], recv, index)
        used.append((buf.at[pl.ds(0, len(devices))], index))

    mask = block_mask(SPAN, SPAN)
    mask_gram = ((iota((2 * ROWS, 2 * ROWS), 0) % ROWS) // NV) == (
        (iota((2 * ROWS, 2 * ROWS), 1) % ROWS) // NV
    )
    section = iota((NV, SPAN), 1) // ROWS

    def grams(left, right):
        full = jnp.where(mask_gram, dot(left, right, nt=True, precision=HIGHEST), 0.0)
        return jnp.concatenate([sum_groups(full[:ROWS]), sum_groups(full[ROWS:])], axis=1)

    def project(block):
        high, low = split(block)
        out = []
        for k in range(LK):
            rows = slice(k * NV, (k + 1) * NV)
            both = jnp.concatenate([block[rows], low[rows].astype(F32)], axis=0).astype(BF16)
            got = dot(both, coeff[k], nt=True)
            out.append(got[:NV] + got[NV:])
        return jnp.concatenate(out, axis=0)

    def section_of(total, which):
        return fold(jnp.where(section == which, total, 0.0)) * (1.0 / count)

    for load in loads[:3]:
        load.wait()
    energy = jnp.concatenate(
        [jnp.broadcast_to(energy_ref[k:k + 1, :], (NV, energy_ref.shape[1])) for k in range(LK)],
        axis=0,
    )
    block = x_ref[...]
    scaled = energy * block
    zeros = jnp.zeros_like(block)
    payload = project(block)
    sums = grams(jnp.concatenate([block, scaled], 0), jnp.concatenate([zeros, block], 0))

    for load in loads[3:5]:
        load.wait()

    def place(k):
        return ((k >> 2) & 1) * half_rows + (k >> 3) * ROWS + (k & 3) * NV

    lane_task = iota((1, half_rows), 1) // NV
    target = jnp.zeros((1, half_rows), jnp.int32)
    pairs = []
    for i in range(TASKS):
        pair = assign_ref[i]
        target = jnp.where(lane_task == i, place(pair >> 6), target)
        pairs.append(jnp.full((NV, SPAN), pair, jnp.int32))
    target = target + iota((1, half_rows), 1) % NV
    e8[...] = (iota((ALL, half_rows), 0) == target).astype(F32).astype(BF16)
    pairs = jnp.concatenate(pairs, axis=0)
    task_row, task_col = pairs >> 6, pairs & 63
    lane = iota((half_rows, SPAN), 1)
    source_row = place(task_col) + iota((half_rows, SPAN), 0) % NV
    for j in range(ALL // SPAN):
        pick[:, j * SPAN:(j + 1) * SPAN] = (lane + j * SPAN == source_row).astype(F32).astype(BF16)
    chosen = dot((lane[:, :GRP * LK] == task_row[:, :GRP * LK]).astype(F32).astype(BF16),
                 ranks_ref[...].astype(F32).astype(BF16))
    chosen = jnp.where(lane[:, :GRP * LK] == task_col[:, :GRP * LK], chosen, 0.0)
    rank = jnp.sum(chosen, axis=1, keepdims=True)
    keep[...] = (iota((half_rows, LEV), 1).astype(F32) < rank).astype(F32)

    pl.semaphore_wait(barrier, len(peers))

    basis = None
    own_energy = None
    for step in range(ITERS):
        d1[step, t, 0:ROWS, :] = payload
        d1[step, t, ROWS:, :] = jnp.concatenate([sums, jnp.zeros_like(sums)], axis=1)
        gather(d1.at[step], t, tiles, 10 * step + 0)
        total = d1[step, 0]
        for i in range(1, TILE):
            total = total + d1[step, i]
        d2[step, core, chip] = total
        gather(d2.at[step, core], chip, chips, 10 * step + 1)
        push(d2.at[step, core], d2.at[step, core], 10 * step + 2, sibling)
        await_bytes(d2.at[step, 0], recv, 10 * step + 2)
        used.append((d2.at[step, 0], 10 * step + 2))

        total = jnp.zeros((NV, SPAN), F32)
        for i in range(CHIPS):
            for c in range(CORES):
                total = total + d2[step, c, i, ROWS:, 0:SPAN]
        pv, pp, rv, rp = [section_of(total, i) for i in range(4)]
        pv_spread = spread(pv, mask)
        if step == 0:
            gram = pp
        else:
            gram = pp - dot(pv, pv_spread, nt=True, precision=HIGHEST)
        inverse = inverse_factor(gram)
        inverse_spread = spread(inverse, mask)
        inv_high, inv_low = split(inverse_spread)
        pv_high, pv_low = split(pv_spread)

        def apply(high, low, rows):
            rows_high, rows_low = split(rows)
            return (
                dot(jnp.concatenate([high, high], axis=1), jnp.concatenate([rows_high, rows_low], axis=0))
                + dot(low, rows_high)
            )

        for j in range(ALL // SPAN):
            raw = jnp.concatenate(
                [d2[step, j // 2, (j % 2) * 4 + i, 0:ROWS, :] for i in range(4)], axis=0
            )
            if step:
                raw = raw - apply(pv_high, pv_low, dens[step - 1, j * SPAN:(j + 1) * SPAN, :])
            dens[step, j * SPAN:(j + 1) * SPAN, :] = apply(inv_high, inv_low, raw)

        if step:
            block = block - dot(pv_spread[:ROWS, :ROWS], basis, precision=HIGHEST)
            crossed = dot(rv, pv_spread, nt=True, precision=HIGHEST)
            crossed_t = dot(pv, spread(rv, mask), nt=True, precision=HIGHEST)
            inner = dot(pv, spread(own_energy, mask), precision=HIGHEST)
            rp = rp - crossed - crossed_t + dot(inner, pv_spread, nt=True, precision=HIGHEST)
        basis = dot(inverse_spread[:ROWS, :ROWS], block, precision=HIGHEST)
        half = dot(inverse, spread(rp, mask), precision=HIGHEST)
        own_energy = dot(half, inverse_spread, nt=True, precision=HIGHEST)

        if step == 0:
            loads[5].wait()
        chosen = dot(pick[...], dens[step].astype(BF16)) * keep[...]
        for i in range(TASKS):
            rows = slice(i * NV, (i + 1) * NV)
            term[rows, :] = dot(chosen[rows].astype(BF16), screen[i], nt=True)
        term_high, term_low = split(term[...] * keep[...])
        part[...] = dot(e8[...], term_high) + dot(e8[...], term_low)
        coupled = jnp.zeros((SPAN, SPAN), F32)
        for j in range(ALL // SPAN):
            rows = slice(j * SPAN, (j + 1) * SPAN)
            coupled = coupled + dot(part[rows, :].astype(BF16), dens[step, rows, :].astype(BF16), nt=True)
        coupled = sum_groups(jnp.where(mask, coupled, 0.0))

        theirs = pl.ds(pl.multiple_of((1 - core) * half_rows, half_rows), half_rows)
        r1s[step] = part[theirs, :].astype(BF16)
        a1s[step] = coupled
        push(r1s.at[step], r1.at[step], 10 * step + 3, sibling)
        push(a1s.at[step], a1.at[step], 10 * step + 4, sibling)
        mine = part[pl.ds(pl.multiple_of(core * half_rows, half_rows), half_rows), :]
        await_bytes(r1.at[step], recv, 10 * step + 3)
        await_bytes(a1.at[step], recv, 10 * step + 4)
        used.append((r1.at[step], 10 * step + 3))
        used.append((a1.at[step], 10 * step + 4))
        summed = (mine + r1[step].astype(F32)).astype(BF16)
        for i in range(CHIPS):
            r2s[step, i] = summed[i * ROWS:(i + 1) * ROWS]
        a2[step, chip] = coupled + a1[step]
        for c, device in zip(chip_ids, chips):
            push(r2s.at[step, c], r2.at[step, chip], 10 * step + 5, device)
        gather_index = 10 * step + 6
        r2[step, chip] = r2s[step, chip]
        gather(a2.at[step], chip, chips, gather_index)
        await_bytes(r2.at[step, pl.ds(0, CHIPS - 1)], recv, 10 * step + 5)
        used.append((r2.at[step, pl.ds(0, CHIPS - 1)], 10 * step + 5))
        rows_sum = r2[step, 0].astype(F32)
        a_sum = a2[step, 0]
        for i in range(1, CHIPS):
            rows_sum = rows_sum + r2[step, i].astype(F32)
            a_sum = a_sum + a2[step, i]
        r3[step, t] = rows_sum.astype(BF16)
        a3[step, t] = a_sum
        for device in tiles:
            push(r3.at[step, t], r3.at[step, t], 10 * step + 7, device)
        gather(a3.at[step], t, tiles, 10 * step + 8)
        await_bytes(r3.at[step, pl.ds(0, TILE - 1)], recv, 10 * step + 7)
        used.append((r3.at[step, pl.ds(0, TILE - 1)], 10 * step + 7))
        rows_sum = r3[step, 0].astype(F32)
        a_sum = a3[step, 0]
        for i in range(1, TILE):
            rows_sum = rows_sum + r3[step, i].astype(F32)
            a_sum = a_sum + a3[step, i]

        ray_t = fold(a_sum) * (1.0 / count) + own_energy
        eye = (iota((NV, SPAN), 0) == iota((NV, SPAN), 1)).astype(F32)
        first = jnp.where(iota((NV, SPAN), 1) < NV, ray_t, 0.0)
        ray_ref[step] = dot(eye, first, nt=True, precision=HIGHEST)
        rows_b = rows_sum.astype(BF16)
        sigma = energy * basis + jnp.concatenate(
            [dot(rows_b[k * NV:(k + 1) * NV], coeff[k]) for k in range(LK)], axis=0
        )
        residual = sigma - dot(spread(ray_t, mask)[:ROWS, :ROWS], basis, precision=HIGHEST)
        block = residual / energy
        sums = grams(
            jnp.concatenate([block, residual], 0), jnp.concatenate([basis, block], 0)
        )
        if step + 1 < ITERS:
            payload = project(block)

    res_ref[...] = residual
    f1[t] = sums
    gather(f1, t, tiles, 10 * ITERS)
    total = f1[0]
    for i in range(1, TILE):
        total = total + f1[i]
    f2[core, chip] = total
    gather(f2.at[core], chip, chips, 10 * ITERS + 1)
    push(f2.at[core], f2.at[core], 10 * ITERS + 2, sibling)
    await_bytes(f2.at[0], recv, 10 * ITERS + 2)
    used.append((f2.at[0], 10 * ITERS + 2))
    total = jnp.zeros((NV, SPAN), F32)
    for i in range(CHIPS):
        for c in range(CORES):
            total = total + f2[c, i]
    pv, pp = section_of(total, 0), section_of(total, 1)
    pv_spread = spread(pv, mask)
    gram = pp - dot(pv, pv_spread, nt=True, precision=HIGHEST)
    inverse_spread = spread(inverse_factor(gram), mask)
    block = block - dot(pv_spread[:ROWS, :ROWS], basis, precision=HIGHEST)
    basis_ref[...] = dot(inverse_spread[:ROWS, :ROWS], block, precision=HIGHEST)

    for ref, index in used:
        await_bytes(ref, send, index)


def per_device(coeff, energy, ranks, assign, screen, initial):
    width = initial.shape[2]
    count = initial.shape[0] * GRP * width * TILE
    vmem = pl.BlockSpec(memory_space=pltpu.VMEM)
    hbm = pl.BlockSpec(memory_space=pltpu.HBM)
    phases = 10 * ITERS + 3
    ray, basis, residual = pl.pallas_call(
        functools.partial(body, count),
        out_shape=[
            jax.ShapeDtypeStruct((ITERS, NV, NV), F32),
            jax.ShapeDtypeStruct((ROWS, width), F32),
            jax.ShapeDtypeStruct((ROWS, width), F32),
        ],
        in_specs=[hbm] * 6,
        out_specs=[vmem, vmem, vmem],
        scratch_shapes=[
            pltpu.VMEM(coeff.shape, BF16),
            pltpu.VMEM(screen.shape, BF16),
            pltpu.VMEM((ITERS, TILE, ROWS + NV, LEV), F32),
            pltpu.VMEM((ITERS, CORES, CHIPS, ROWS + NV, LEV), F32),
            pltpu.VMEM((ITERS, ALL, LEV), F32),
            pltpu.VMEM((ALL // 2, LEV), F32),
            pltpu.VMEM((ALL, LEV), F32),
            pltpu.VMEM((ALL, ALL // 2), BF16),
            pltpu.VMEM((ALL // 2, ALL), BF16),
            pltpu.VMEM((ALL // 2, LEV), F32),
            pltpu.VMEM((ITERS, ALL // 2, LEV), BF16),
            pltpu.VMEM((ITERS, ALL // 2, LEV), BF16),
            pltpu.VMEM((ITERS, NV, SPAN), F32),
            pltpu.VMEM((ITERS, NV, SPAN), F32),
            pltpu.VMEM((ITERS, CHIPS, ROWS, LEV), BF16),
            pltpu.VMEM((ITERS, CHIPS, ROWS, LEV), BF16),
            pltpu.VMEM((ITERS, CHIPS, NV, SPAN), F32),
            pltpu.VMEM((ITERS, TILE, ROWS, LEV), BF16),
            pltpu.VMEM((ITERS, TILE, NV, SPAN), F32),
            pltpu.VMEM((TILE, NV, SPAN), F32),
            pltpu.VMEM((CORES, CHIPS, NV, SPAN), F32),
            pltpu.SMEM(assign.shape, jnp.int32),
            pltpu.VMEM(ranks.shape, jnp.int32),
            pltpu.VMEM(energy.shape, F32),
            pltpu.VMEM((ROWS, width), F32),
            pltpu.SemaphoreType.DMA((6,)),
            pltpu.SemaphoreType.DMA((phases,)),
            pltpu.SemaphoreType.DMA((phases,)),
        ],
        compiler_params=pltpu.CompilerParams(
            collective_id=0, has_side_effects=True, vmem_limit_bytes=54 * 2**20
        ),
        name="davidson",
    )(assign, ranks, coeff, screen, energy, initial.reshape(ROWS, width))
    return ray, basis.reshape(initial.shape), residual.reshape(initial.shape)


def solution(mesh):
    placed = (
        P("grp", None, "tile"),
        P("grp", "tile"),
        P(),
        P(("grp", "tile")),
        P(("grp", "tile"), None, None),
        P("grp", None, "tile"),
    )
    return jax.shard_map(
        per_device,
        mesh=mesh,
        in_specs=placed,
        out_specs=(P(), P("grp", None, "tile"), P("grp", None, "tile")),
        check_vma=False,
    )
```

```python
import functools

import jax
import jax.numpy as jnp
from jax import lax
from jax.experimental import pallas as pl
from jax.experimental.pallas import tpu as pltpu
from jax.sharding import PartitionSpec as P

ITERS = 2
NV = 8
GRP, TILE, CHIPS, CORES = 16, 8, 8, 2
LK = 4
ROWS = LK * NV
ALL = GRP * ROWS
LEV = 256
TASKS = 32
SEMS = 64
SPAN = 128
F32, BF16 = jnp.float32, jnp.bfloat16
HIGHEST = lax.Precision.HIGHEST
MESH = pl.DeviceIdType.MESH
CHIP_STEPS = ((1, 2), (0, 2), (1, 1), (1, 3), (0, 1), (0, 3), (1, 0))
TILE_STEPS = ((1, 2), (1, 1), (1, 3), (1, 0), (0, 2), (0, 1), (0, 3))


def dot(a, b, nt=False, precision=None):
    return lax.dot_general(
        a, b, (((1,), (1 if nt else 0,)), ((), ())),
        precision=precision, preferred_element_type=F32,
    )


def split(a):
    high = a.astype(BF16)
    return high, (a - high.astype(F32)).astype(BF16)


def iota(shape, dim):
    return lax.broadcasted_iota(jnp.int32, shape, dim)


def block_mask(rows, cols):
    return (iota((rows, cols), 0) // NV) == (iota((rows, cols), 1) // NV)


def fold(part):
    for step in (8, 16, 32, 64):
        part = part + pltpu.roll(part, step, 1)
    return part


def sum_groups(a):
    total = a[0:NV]
    for i in range(1, a.shape[0] // NV):
        total = total + a[i * NV:(i + 1) * NV]
    return total


def spread(small, mask):
    return jnp.where(mask, jnp.concatenate([small] * (SPAN // NV), axis=0), 0.0)


def inverse_factor(gram):
    sub, lane = iota((NV, SPAN), 0), iota((NV, SPAN), 1) % NV
    right = (sub == lane).astype(F32)
    pivots = jnp.ones((NV, SPAN), F32)
    for j in range(NV):
        row, other = gram[j:j + 1, :], right[j:j + 1, :]
        pivot = jnp.broadcast_to(row[:, j:j + 1], (NV, SPAN))
        pivots = jnp.where(sub == j, pivot, pivots)
        factor = jnp.broadcast_to(gram[:, j:j + 1], (NV, SPAN)) / pivot
        factor = jnp.where(sub > j, factor, 0.0)
        gram = gram - factor * row
        right = right - factor * other
    return right * lax.rsqrt(pivots)


def body(
    count, assign_hbm, ranks_hbm, coeff_hbm, screen_hbm, energy_hbm, x_hbm,
    ray_ref, basis_ref, res_ref,
    coeff, screen, g1, g2, d1, d2, dens, dens_b, term, e8, pick, keep,
    r1s, r1, a1s, a1, r2s, r2, a2, r3, a3, f1, f2,
    assign_ref, ranks_ref, energy_ref, x_ref, load_sem, send, recv,
):
    g, t = lax.axis_index("grp"), lax.axis_index("tile")
    core, chip = lax.rem(g, CORES), lax.div(g, CORES)
    y_lo, x = lax.div(chip, 4), lax.rem(chip, 4)
    y_hi, z = lax.div(t, 4), lax.rem(t, 4)
    sibling = (chip * CORES + (1 - core), t)
    to_ids = [lax.rem(y_lo + a, 2) * 4 + lax.rem(x + b, 4) for a, b in CHIP_STEPS]
    from_ids = [lax.rem(y_lo + 2 - a, 2) * 4 + lax.rem(x + 4 - b, 4) for a, b in CHIP_STEPS]
    chips = [(c * CORES + core, t) for c in to_ids]
    tiles = [(g, lax.rem(y_hi + a, 2) * 4 + lax.rem(z + b, 4)) for a, b in TILE_STEPS]

    half_rows = ALL // 2
    barrier = pltpu.get_barrier_semaphore()
    peers = [*tiles, *chips, sibling]
    for peer in peers:
        pl.semaphore_signal(barrier, inc=1, device_id=peer, device_id_type=MESH)
    loads = [
        pltpu.make_async_copy(src, dst, load_sem.at[i])
        for i, (src, dst) in enumerate((
            (x_hbm, x_ref), (energy_hbm, energy_ref), (coeff_hbm, coeff),
            (assign_hbm, assign_ref), (ranks_hbm, ranks_ref), (screen_hbm, screen),
        ))
    ]
    for load in loads:
        load.start()

    used = []
    numbers = iter(range(SEMS))

    def push(src, dst, index, device):
        pltpu.make_async_remote_copy(
            src_ref=src, dst_ref=dst, send_sem=send.at[index], recv_sem=recv.at[index],
            device_id=device, device_id_type=MESH,
        ).start()

    def await_bytes(ref, sems, index):
        pltpu.make_async_copy(ref, ref, sems.at[index]).wait()

    def offer(buf, mine, devices):
        index = next(numbers)
        for device in devices:
            push(buf.at[mine], buf.at[mine], index, device)
        size = buf.at[pl.ds(0, len(devices))]
        used.append((size, index))
        return lambda: await_bytes(size, recv, index)

    def hand(src, dst):
        index = next(numbers)
        push(src, dst, index, sibling)
        used.append((dst, index))
        return lambda: await_bytes(dst, recv, index)

    def add_up(buf, n):
        total = buf[0].astype(F32)
        for i in range(1, n):
            total = total + buf[i].astype(F32)
        return total

    mask = block_mask(SPAN, SPAN)
    mask_gram = ((iota((2 * ROWS, 2 * ROWS), 0) % ROWS) // NV) == (
        (iota((2 * ROWS, 2 * ROWS), 1) % ROWS) // NV
    )
    section = iota((NV, SPAN), 1) // ROWS

    def grams(left, right):
        full = jnp.where(mask_gram, dot(left, right, nt=True, precision=HIGHEST), 0.0)
        return jnp.concatenate([sum_groups(full[:ROWS]), sum_groups(full[ROWS:])], axis=1)

    def project(block):
        low = block - block.astype(BF16).astype(F32)
        out = []
        for k in range(LK):
            rows = slice(k * NV, (k + 1) * NV)
            both = jnp.concatenate([block[rows], low[rows]], axis=0).astype(BF16)
            got = dot(both, coeff[k], nt=True)
            out.append(got[:NV] + got[NV:])
        return jnp.concatenate(out, axis=0)

    def section_of(total, which):
        return fold(jnp.where(section == which, total, 0.0)) * (1.0 / count)

    def place(k):
        return ((k >> 2) & 1) * half_rows + (k >> 3) * ROWS + (k & 3) * NV

    def one_hots():
        for load in loads[3:5]:
            load.wait()
        lane_task = iota((1, half_rows), 1) // NV
        target = jnp.zeros((1, half_rows), jnp.int32)
        pairs = []
        for i in range(TASKS):
            pair = assign_ref[i]
            target = jnp.where(lane_task == i, place(pair >> 6), target)
            pairs.append(jnp.full((NV, SPAN), pair, jnp.int32))
        target = target + iota((1, half_rows), 1) % NV
        e8[...] = (iota((ALL, half_rows), 0) == target).astype(F32).astype(BF16)
        pairs = jnp.concatenate(pairs, axis=0)
        task_row, task_col = pairs >> 6, pairs & 63
        lane = iota((half_rows, SPAN), 1)
        source_row = place(task_col) + iota((half_rows, SPAN), 0) % NV
        for j in range(ALL // SPAN):
            pick[:, j * SPAN:(j + 1) * SPAN] = (
                (lane + j * SPAN == source_row).astype(F32).astype(BF16)
            )
        k_points = GRP * LK
        chosen = dot((lane[:, :k_points] == task_row[:, :k_points]).astype(F32).astype(BF16),
                     ranks_ref[...].astype(F32).astype(BF16))
        chosen = jnp.where(lane[:, :k_points] == task_col[:, :k_points], chosen, 0.0)
        rank = jnp.sum(chosen, axis=1, keepdims=True)
        keep[...] = (iota((half_rows, LEV), 1).astype(F32) < rank).astype(F32)

    def apply(high, low, rows):
        rows_high, rows_low = split(rows)
        return (
            dot(jnp.concatenate([high, high], axis=1), jnp.concatenate([rows_high, rows_low], axis=0))
            + dot(low, rows_high)
        )

    for load in loads[:2]:
        load.wait()
    energy = jnp.concatenate(
        [jnp.broadcast_to(energy_ref[k:k + 1, :], (NV, energy_ref.shape[1])) for k in range(LK)],
        axis=0,
    )
    block = x_ref[...]
    zeros = jnp.zeros_like(block)
    sums = grams(jnp.concatenate([block, energy * block], 0), jnp.concatenate([zeros, block], 0))
    loads[2].wait()
    payload = project(block)
    pl.semaphore_wait(barrier, len(peers))

    basis = None
    own_energy = None
    residual = None
    mine = pl.ds(pl.multiple_of(core * half_rows, half_rows), half_rows)
    theirs = pl.ds(pl.multiple_of((1 - core) * half_rows, half_rows), half_rows)
    for step in range(ITERS):
        g1[step, t] = sums
        wait_g1 = offer(g1.at[step], t, tiles)
        if step:
            payload = project(block)
        d1[step, t] = payload
        wait_d1 = offer(d1.at[step], t, tiles)
        if step == 0:
            one_hots()
        wait_g1()
        g2[step, core, chip] = add_up(g1.at[step], TILE)
        wait_g2 = offer(g2.at[step, core], chip, chips)
        wait_d1()
        d2[step, core, chip] = add_up(d1.at[step], TILE)
        mine_now = d2.at[step, core, chip]
        arrivals = [next(numbers) for _ in chips]
        for index, device in zip(arrivals, chips):
            push(mine_now, mine_now, index, device)
            used.append((mine_now, index))
        pass_on = next(numbers)
        push(mine_now, mine_now, pass_on, sibling)
        wait_g2()
        hand(g2.at[step, core], g2.at[step, core])()

        total = jnp.zeros((NV, SPAN), F32)
        for i in range(CHIPS):
            for c in range(CORES):
                total = total + g2[step, c, i]
        pv, pp, rv, rp = [section_of(total, i) for i in range(4)]
        pv_spread = spread(pv, mask)
        gram = pp
        if step:
            gram = pp - dot(pv, pv_spread, nt=True, precision=HIGHEST)
        inverse = inverse_factor(gram)
        inverse_spread = spread(inverse, mask)
        inv_high, inv_low = split(inverse_spread)
        pv_high, pv_low = split(pv_spread)

        for index, source in reversed(list(zip(arrivals, from_ids))):
            landed = d2.at[step, core, source]
            await_bytes(landed, recv, index)
            push(landed, landed, pass_on, sibling)
        whole = d2.at[step, 0]
        used.append((whole, pass_on))
        await_bytes(whole, recv, pass_on)
        for j in range(ALL // SPAN):
            rows = slice(j * SPAN, (j + 1) * SPAN)
            raw = jnp.concatenate(
                [d2[step, j // 2, (j % 2) * 4 + i] for i in range(4)], axis=0
            )
            if step:
                raw = raw - apply(pv_high, pv_low, dens[rows, :])
            raw = apply(inv_high, inv_low, raw)
            dens_b[rows, :] = raw.astype(BF16)
            if step + 1 < ITERS:
                dens[rows, :] = raw

        if step == 0:
            loads[5].wait()
        chosen = dot(pick[...], dens_b[...]) * keep[...]
        for i in range(TASKS):
            rows = slice(i * NV, (i + 1) * NV)
            term[rows, :] = dot(chosen[rows].astype(BF16), screen[i], nt=True)
        term_high, term_low = split(term[...] * keep[...])

        r1s[step] = (dot(e8[theirs, :], term_high) + dot(e8[theirs, :], term_low)).astype(BF16)
        wait_r1 = hand(r1s.at[step], r1.at[step])
        own = dot(e8[mine, :], term_high) + dot(e8[mine, :], term_low)
        own_b = own.astype(BF16)
        coupled = jnp.zeros((SPAN, SPAN), F32)
        for j in range(half_rows // SPAN):
            rows = slice(j * SPAN, (j + 1) * SPAN)
            coupled = coupled + dot(r1s[step, rows, :], dens_b[theirs, :][rows], nt=True)
            coupled = coupled + dot(own_b[rows], dens_b[mine, :][rows], nt=True)
        coupled = sum_groups(jnp.where(mask, coupled, 0.0))
        a1s[step] = coupled
        wait_a1 = hand(a1s.at[step], a1.at[step])
        wait_r1()
        summed = (own + r1[step].astype(F32)).astype(BF16)
        for i in range(CHIPS):
            r2s[step, i] = summed[i * ROWS:(i + 1) * ROWS]
        r2_index = next(numbers)
        for c, device in zip(to_ids, chips):
            push(r2s.at[step, c], r2.at[step, chip], r2_index, device)
        r2[step, chip] = r2s[step, chip]
        r2_size = r2.at[step, pl.ds(0, CHIPS - 1)]
        used.append((r2_size, r2_index))
        wait_a1()
        a2[step, chip] = coupled + a1[step]
        wait_a2 = offer(a2.at[step], chip, chips)

        if step:
            block = block - dot(pv_spread[:ROWS, :ROWS], basis, precision=HIGHEST)
            crossed = dot(rv, pv_spread, nt=True, precision=HIGHEST)
            crossed_t = dot(pv, spread(rv, mask), nt=True, precision=HIGHEST)
            inner = dot(pv, spread(own_energy, mask), precision=HIGHEST)
            rp = rp - crossed - crossed_t + dot(inner, pv_spread, nt=True, precision=HIGHEST)
        basis = dot(inverse_spread[:ROWS, :ROWS], block, precision=HIGHEST)
        half = dot(inverse, spread(rp, mask), precision=HIGHEST)
        own_energy = dot(half, inverse_spread, nt=True, precision=HIGHEST)

        await_bytes(r2_size, recv, r2_index)
        r3[step, t] = add_up(r2.at[step], CHIPS).astype(BF16)
        wait_r3 = offer(r3.at[step], t, tiles)
        wait_a2()
        a3[step, t] = add_up(a2.at[step], CHIPS)
        wait_a3 = offer(a3.at[step], t, tiles)
        wait_r3()
        rows_b = add_up(r3.at[step], TILE).astype(BF16)
        sigma = energy * basis + jnp.concatenate(
            [dot(rows_b[k * NV:(k + 1) * NV], coeff[k]) for k in range(LK)], axis=0
        )
        wait_a3()
        ray_t = fold(add_up(a3.at[step], TILE)) * (1.0 / count) + own_energy
        residual = sigma - dot(spread(ray_t, mask)[:ROWS, :ROWS], basis, precision=HIGHEST)
        block = residual / energy
        sums = grams(
            jnp.concatenate([block, residual], 0), jnp.concatenate([basis, block], 0)
        )
        eye = (iota((NV, SPAN), 0) == iota((NV, SPAN), 1)).astype(F32)
        first = jnp.where(iota((NV, SPAN), 1) < NV, ray_t, 0.0)
        ray_ref[step] = dot(eye, first, nt=True, precision=HIGHEST)

    f1[t] = sums
    wait_f1 = offer(f1, t, tiles)
    res_ref[...] = residual
    wait_f1()
    f2[core, chip] = add_up(f1, TILE)
    offer(f2.at[core], chip, chips)()
    hand(f2.at[core], f2.at[core])()
    total = jnp.zeros((NV, SPAN), F32)
    for i in range(CHIPS):
        for c in range(CORES):
            total = total + f2[c, i]
    pv, pp = section_of(total, 0), section_of(total, 1)
    pv_spread = spread(pv, mask)
    gram = pp - dot(pv, pv_spread, nt=True, precision=HIGHEST)
    inverse_spread = spread(inverse_factor(gram), mask)
    block = block - dot(pv_spread[:ROWS, :ROWS], basis, precision=HIGHEST)
    basis_ref[...] = dot(inverse_spread[:ROWS, :ROWS], block, precision=HIGHEST)

    for ref, index in used:
        await_bytes(ref, send, index)


def hand_out(ray, basis, residual, ray_out, basis_out, residual_out):
    basis_out[...] = basis[...]
    residual_out[...] = residual[...]
    ray_out[...] = ray[...]


def per_device(coeff, energy, ranks, assign, screen, initial):
    width = initial.shape[2]
    count = initial.shape[0] * GRP * width * TILE
    vmem = pl.BlockSpec(memory_space=pltpu.VMEM)
    hbm = pl.BlockSpec(memory_space=pltpu.HBM)
    ray, basis, residual = pl.pallas_call(
        functools.partial(body, count),
        out_shape=[
            jax.ShapeDtypeStruct((ITERS, NV, NV), F32),
            jax.ShapeDtypeStruct((ROWS, width), F32),
            jax.ShapeDtypeStruct((ROWS, width), F32),
        ],
        in_specs=[hbm] * 6,
        out_specs=[vmem, vmem, vmem],
        scratch_shapes=[
            pltpu.VMEM(coeff.shape, BF16),
            pltpu.VMEM(screen.shape, BF16),
            pltpu.VMEM((ITERS, TILE, NV, SPAN), F32),
            pltpu.VMEM((ITERS, CORES, CHIPS, NV, SPAN), F32),
            pltpu.VMEM((ITERS, TILE, ROWS, LEV), F32),
            pltpu.VMEM((ITERS, CORES, CHIPS, ROWS, LEV), F32),
            pltpu.VMEM((ALL, LEV), F32),
            pltpu.VMEM((ALL, LEV), BF16),
            pltpu.VMEM((ALL // 2, LEV), F32),
            pltpu.VMEM((ALL, ALL // 2), BF16),
            pltpu.VMEM((ALL // 2, ALL), BF16),
            pltpu.VMEM((ALL // 2, LEV), F32),
            pltpu.VMEM((ITERS, ALL // 2, LEV), BF16),
            pltpu.VMEM((ITERS, ALL // 2, LEV), BF16),
            pltpu.VMEM((ITERS, NV, SPAN), F32),
            pltpu.VMEM((ITERS, NV, SPAN), F32),
            pltpu.VMEM((ITERS, CHIPS, ROWS, LEV), BF16),
            pltpu.VMEM((ITERS, CHIPS, ROWS, LEV), BF16),
            pltpu.VMEM((ITERS, CHIPS, NV, SPAN), F32),
            pltpu.VMEM((ITERS, TILE, ROWS, LEV), BF16),
            pltpu.VMEM((ITERS, TILE, NV, SPAN), F32),
            pltpu.VMEM((TILE, NV, SPAN), F32),
            pltpu.VMEM((CORES, CHIPS, NV, SPAN), F32),
            pltpu.SMEM(assign.shape, jnp.int32),
            pltpu.VMEM(ranks.shape, jnp.int32),
            pltpu.VMEM(energy.shape, F32),
            pltpu.VMEM((ROWS, width), F32),
            pltpu.SemaphoreType.DMA((6,)),
            pltpu.SemaphoreType.DMA((SEMS,)),
            pltpu.SemaphoreType.DMA((SEMS,)),
        ],
        compiler_params=pltpu.CompilerParams(
            collective_id=0, has_side_effects=True, vmem_limit_bytes=32 * 2**20
        ),
        name="davidson",
    )(*[pltpu.with_memory_space_constraint(a, pltpu.HBM) for a in (assign, ranks, coeff, screen, energy, initial.reshape(ROWS, width))])
    basis, residual = basis.reshape(initial.shape), residual.reshape(initial.shape)
    results = (ray, basis, residual)
    return tuple(pl.pallas_call(
        hand_out,
        out_shape=[jax.ShapeDtypeStruct(r.shape, r.dtype) for r in results],
        in_specs=[vmem] * 3,
        out_specs=[vmem] * 3,
        compiler_params=pltpu.CompilerParams(vmem_limit_bytes=8 * 2**20),
        name="hand_out",
    )(*results))


def solution(mesh):
    placed = (
        P("grp", None, "tile"),
        P("grp", "tile"),
        P(),
        P(("grp", "tile")),
        P(("grp", "tile"), None, None),
        P("grp", None, "tile"),
    )
    return jax.shard_map(
        per_device,
        mesh=mesh,
        in_specs=placed,
        out_specs=(P(), P("grp", None, "tile"), P("grp", None, "tile")),
        check_vma=False,
    )
```

```python
import functools

import jax
import jax.numpy as jnp
from jax import lax
from jax.experimental import pallas as pl
from jax.experimental.pallas import tpu as pltpu
from jax.sharding import PartitionSpec as P

ITERS = 2
NV = 8
GRP, TILE, CHIPS, CORES = 16, 8, 8, 2
LK = 4
ROWS = LK * NV
ALL = GRP * ROWS
LEV = 256
TASKS = 32
SEMS = 64
SPAN = 128
F32, BF16 = jnp.float32, jnp.bfloat16
HIGHEST = lax.Precision.HIGHEST
MESH = pl.DeviceIdType.MESH
CHIP_STEPS = ((1, 2), (0, 2), (1, 1), (1, 3), (0, 1), (0, 3), (1, 0))
TILE_STEPS = ((1, 2), (1, 1), (1, 3), (1, 0), (0, 2), (0, 1), (0, 3))


def dot(a, b, nt=False, precision=None):
    return lax.dot_general(
        a, b, (((1,), (1 if nt else 0,)), ((), ())),
        precision=precision, preferred_element_type=F32,
    )


def split(a):
    high = a.astype(BF16)
    return high, (a - high.astype(F32)).astype(BF16)


def iota(shape, dim):
    return lax.broadcasted_iota(jnp.int32, shape, dim)


def block_mask(rows, cols):
    return (iota((rows, cols), 0) // NV) == (iota((rows, cols), 1) // NV)


def fold(part):
    for step in (8, 16, 32, 64):
        part = part + pltpu.roll(part, step, 1)
    return part


def sum_groups(a):
    total = a[0:NV]
    for i in range(1, a.shape[0] // NV):
        total = total + a[i * NV:(i + 1) * NV]
    return total


def spread(small, mask):
    return jnp.where(mask, jnp.concatenate([small] * (SPAN // NV), axis=0), 0.0)


def factor(gram, ridge=False):
    whole = (NV, SPAN)
    columns = [jnp.broadcast_to(gram[:, m:m + 1], whole) for m in range(NV)]
    e = [[jnp.broadcast_to(columns[m][n:n + 1, :], whole) for m in range(n + 1)] for n in range(NV)]
    if ridge:
        trace = e[0][0]
        for n in range(1, NV):
            trace = trace + e[n][n]
        for n in range(NV):
            e[n][n] = e[n][n] + (trace * 1e-6 + 1e-30)
    unit = [[None] * NV for _ in range(NV)]
    for j in range(NV):
        inverse_pivot = 1.0 / e[j][j]
        for i in range(j + 1, NV):
            unit[i][j] = e[i][j] * inverse_pivot
            for m in range(j + 1, i + 1):
                e[i][m] = e[i][m] - unit[i][j] * e[m][j]
    back = [[None] * NV for _ in range(NV)]
    for j in range(NV):
        for i in range(j + 1, NV):
            value = unit[i][j]
            for q in range(j + 1, i):
                value = value + unit[i][q] * back[q][j]
            back[i][j] = -value
    scale = [lax.rsqrt(e[n][n]) for n in range(NV)]
    root = [e[n][n] * scale[n] for n in range(NV)]
    sub, lane = iota(whole, 0), iota(whole, 1) % NV

    def assemble(entry):
        out = jnp.zeros(whole, F32)
        for i in range(NV):
            row = jnp.zeros(whole, F32)
            for j in range(i + 1):
                row = jnp.where(lane == j, entry(i, j), row)
            out = jnp.where(sub == i, row, out)
        return out

    inverse = assemble(lambda i, j: scale[i] if i == j else scale[i] * back[i][j])
    lower = assemble(lambda i, j: root[i] if i == j else unit[i][j] * root[j])
    return inverse, lower


def body(
    count, assign_hbm, ranks_hbm, coeff_hbm, screen_hbm, energy_hbm, x_hbm,
    ray_ref, basis_ref, res_ref,
    coeff, screen, g1, g2, t2, d1, d2, dens, dens_b, term, e8, pick, keep,
    r1s, r1, a1s, a1, r2s, r2, a2, r3, a3, f1, f2,
    assign_ref, ranks_ref, energy_ref, x_ref, load_sem, send, recv,
):
    g, t = lax.axis_index("grp"), lax.axis_index("tile")
    core, chip = lax.rem(g, CORES), lax.div(g, CORES)
    y_lo, x = lax.div(chip, 4), lax.rem(chip, 4)
    y_hi, z = lax.div(t, 4), lax.rem(t, 4)
    sibling = (chip * CORES + (1 - core), t)
    to_ids = [lax.rem(y_lo + a, 2) * 4 + lax.rem(x + b, 4) for a, b in CHIP_STEPS]
    from_ids = [lax.rem(y_lo + 2 - a, 2) * 4 + lax.rem(x + 4 - b, 4) for a, b in CHIP_STEPS]
    chips = [(c * CORES + core, t) for c in to_ids]
    tiles = [(g, lax.rem(y_hi + a, 2) * 4 + lax.rem(z + b, 4)) for a, b in TILE_STEPS]

    half_rows = ALL // 2
    barrier = pltpu.get_barrier_semaphore()
    peers = [*tiles, *chips, sibling]
    for peer in peers:
        pl.semaphore_signal(barrier, inc=1, device_id=peer, device_id_type=MESH)
    loads = [
        pltpu.make_async_copy(src, dst, load_sem.at[i])
        for i, (src, dst) in enumerate((
            (x_hbm, x_ref), (energy_hbm, energy_ref), (coeff_hbm, coeff),
            (assign_hbm, assign_ref), (ranks_hbm, ranks_ref), (screen_hbm, screen),
        ))
    ]
    for load in loads:
        load.start()

    used = []
    numbers = iter(range(SEMS))

    def push(src, dst, index, device):
        pltpu.make_async_remote_copy(
            src_ref=src, dst_ref=dst, send_sem=send.at[index], recv_sem=recv.at[index],
            device_id=device, device_id_type=MESH,
        ).start()

    def await_bytes(ref, sems, index):
        pltpu.make_async_copy(ref, ref, sems.at[index]).wait()

    def offer(buf, mine, devices):
        index = next(numbers)
        for device in devices:
            push(buf.at[mine], buf.at[mine], index, device)
        size = buf.at[pl.ds(0, len(devices))]
        used.append((size, index))
        return lambda: await_bytes(size, recv, index)

    def hand(src, dst):
        index = next(numbers)
        push(src, dst, index, sibling)
        used.append((dst, index))
        return lambda: await_bytes(dst, recv, index)

    def add_up(buf, n):
        total = buf[0].astype(F32)
        for i in range(1, n):
            total = total + buf[i].astype(F32)
        return total

    mask = block_mask(SPAN, SPAN)
    mask_gram = ((iota((2 * ROWS, 2 * ROWS), 0) % ROWS) // NV) == (
        (iota((2 * ROWS, 2 * ROWS), 1) % ROWS) // NV
    )
    section = iota((NV, SPAN), 1) // ROWS

    def grams(left, right):
        full = jnp.where(mask_gram, dot(left, right, nt=True, precision=HIGHEST), 0.0)
        return jnp.concatenate([sum_groups(full[:ROWS]), sum_groups(full[ROWS:])], axis=1)

    def by_k_point(block, nt):
        low = block - block.astype(BF16).astype(F32)
        out = []
        for k in range(LK):
            rows = slice(k * NV, (k + 1) * NV)
            both = jnp.concatenate([block[rows], low[rows]], axis=0).astype(BF16)
            got = dot(both, coeff[k], nt=nt)
            out.append(got[:NV] + got[NV:])
        return jnp.concatenate(out, axis=0)

    def section_of(total, which):
        return fold(jnp.where(section == which, total, 0.0)) * (1.0 / count)

    def place(k):
        return ((k >> 2) & 1) * half_rows + (k >> 3) * ROWS + (k & 3) * NV

    def one_hots():
        for load in loads[3:5]:
            load.wait()
        lane_task = iota((1, half_rows), 1) // NV
        target = jnp.zeros((1, half_rows), jnp.int32)
        pairs = []
        for i in range(TASKS):
            pair = assign_ref[i]
            target = jnp.where(lane_task == i, place(pair >> 6), target)
            pairs.append(jnp.full((NV, SPAN), pair, jnp.int32))
        target = target + iota((1, half_rows), 1) % NV
        e8[...] = (iota((ALL, half_rows), 0) == target).astype(F32).astype(BF16)
        pairs = jnp.concatenate(pairs, axis=0)
        task_row, task_col = pairs >> 6, pairs & 63
        lane = iota((half_rows, SPAN), 1)
        source_row = place(task_col) + iota((half_rows, SPAN), 0) % NV
        for j in range(ALL // SPAN):
            pick[:, j * SPAN:(j + 1) * SPAN] = (
                (lane + j * SPAN == source_row).astype(F32).astype(BF16)
            )
        k_points = GRP * LK
        chosen = dot((lane[:, :k_points] == task_row[:, :k_points]).astype(F32).astype(BF16),
                     ranks_ref[...].astype(F32).astype(BF16))
        chosen = jnp.where(lane[:, :k_points] == task_col[:, :k_points], chosen, 0.0)
        rank = jnp.sum(chosen, axis=1, keepdims=True)
        keep[...] = (iota((half_rows, LEV), 1).astype(F32) < rank).astype(F32)

    def apply(high, low, rows):
        rows_high, rows_low = split(rows)
        return (
            dot(jnp.concatenate([high, high], axis=1), jnp.concatenate([rows_high, rows_low], axis=0))
            + dot(low, rows_high)
        )

    for load in loads[:2]:
        load.wait()
    energy = jnp.concatenate(
        [jnp.broadcast_to(energy_ref[k:k + 1, :], (NV, energy_ref.shape[1])) for k in range(LK)],
        axis=0,
    )
    block = x_ref[...]
    zeros = jnp.zeros_like(block)
    sums = grams(jnp.concatenate([block, energy * block], 0), jnp.concatenate([zeros, block], 0))
    loads[2].wait()
    payload = by_k_point(block, True)
    pl.semaphore_wait(barrier, len(peers))

    basis = None
    own_energy = None
    residual = None
    mine = pl.ds(pl.multiple_of(core * half_rows, half_rows), half_rows)
    theirs = pl.ds(pl.multiple_of((1 - core) * half_rows, half_rows), half_rows)
    for step in range(ITERS):
        g1[step, t] = sums
        wait_g1 = offer(g1.at[step], t, tiles)
        if step:
            payload = by_k_point(block, True)
        d1[step, t] = payload
        wait_d1 = offer(d1.at[step], t, tiles)
        if step == 0:
            one_hots()
        wait_g1()
        total = add_up(g1.at[step], TILE)
        g2[step, core, chip] = total
        wait_g2 = offer(g2.at[step, core], chip, chips)
        own_inverse, own_factor = factor(section_of(total, 1), ridge=True)
        t2[step, core, chip] = own_factor
        wait_t2 = offer(t2.at[step, core], chip, chips)
        own_inverse = spread(own_inverse, mask)[:ROWS, :ROWS]
        wait_d1()
        total = add_up(d1.at[step], TILE)
        d2[step, core, chip] = dot(own_inverse, total, precision=HIGHEST).astype(BF16)
        mine_now = d2.at[step, core, chip]
        arrivals = [next(numbers) for _ in chips]
        for index, device in zip(arrivals, chips):
            push(mine_now, mine_now, index, device)
            used.append((mine_now, index))
        pass_on = next(numbers)
        push(mine_now, mine_now, pass_on, sibling)
        wait_g2()
        wait_h2 = hand(g2.at[step, core], g2.at[step, core])
        wait_t2()
        wait_u2 = hand(t2.at[step, core], t2.at[step, core])
        wait_h2()
        total = jnp.zeros((NV, SPAN), F32)
        for i in range(CHIPS):
            for c in range(CORES):
                total = total + g2[step, c, i]
        pv, pp = section_of(total, 0), section_of(total, 1)
        pv_spread = spread(pv, mask)
        gram = pp
        if step:
            gram = pp - dot(pv, pv_spread, nt=True, precision=HIGHEST)
        inverse, _ = factor(gram)
        inverse_spread = spread(inverse, mask)
        wait_u2()
        columns = [jnp.broadcast_to(inverse[:, m:m + 1], (NV, SPAN)) for m in range(NV)]
        mixers = []
        for j in range(ALL // SPAN):
            parts = []
            for i in range(4):
                theirs_t = t2[step, j // 2, (j % 2) * 4 + i]
                mixed = columns[0] * theirs_t[0:1, :]
                for m in range(1, NV):
                    mixed = mixed + columns[m] * theirs_t[m:m + 1, :]
                parts += [mixed] * LK
            mixers.append(split(jnp.where(mask, jnp.concatenate(parts, axis=0), 0.0)))
        if step:
            old = dot(inverse, pv_spread, precision=HIGHEST)
            old_high, old_low = split(spread(old, mask))
            for j in range(ALL // SPAN):
                rows = slice(j * SPAN, (j + 1) * SPAN)
                dens[rows, :] = apply(old_high, old_low, dens[rows, :])

        for index, source in reversed(list(zip(arrivals, from_ids))):
            landed = d2.at[step, core, source]
            await_bytes(landed, recv, index)
            push(landed, landed, pass_on, sibling)
        whole = d2.at[step, 0]
        used.append((whole, pass_on))
        await_bytes(whole, recv, pass_on)
        for j in range(ALL // SPAN):
            rows = slice(j * SPAN, (j + 1) * SPAN)
            landed = jnp.concatenate(
                [d2[step, j // 2, (j % 2) * 4 + i] for i in range(4)], axis=0
            )
            mixed = dot(mixers[j][0], landed) + dot(mixers[j][1], landed)
            if step:
                mixed = mixed - dens[rows, :]
            dens_b[rows, :] = mixed.astype(BF16)
            if step + 1 < ITERS:
                dens[rows, :] = mixed

        if step == 0:
            loads[5].wait()
        chosen = dot(pick[...], dens_b[...]) * keep[...]
        for i in range(TASKS):
            rows = slice(i * NV, (i + 1) * NV)
            term[rows, :] = dot(chosen[rows].astype(BF16), screen[i], nt=True)
        term_high, term_low = split(term[...] * keep[...])

        r1s[step] = (dot(e8[theirs, :], term_high) + dot(e8[theirs, :], term_low)).astype(BF16)
        wait_r1 = hand(r1s.at[step], r1.at[step])
        own = dot(e8[mine, :], term_high) + dot(e8[mine, :], term_low)
        own_b = own.astype(BF16)
        coupled = jnp.zeros((SPAN, SPAN), F32)
        for j in range(half_rows // SPAN):
            rows = slice(j * SPAN, (j + 1) * SPAN)
            coupled = coupled + dot(r1s[step, rows, :], dens_b[theirs, :][rows], nt=True)
            coupled = coupled + dot(own_b[rows], dens_b[mine, :][rows], nt=True)
        coupled = sum_groups(jnp.where(mask, coupled, 0.0))
        a1s[step] = coupled
        wait_a1 = hand(a1s.at[step], a1.at[step])
        wait_r1()
        summed = (own + r1[step].astype(F32)).astype(BF16)
        for i in range(CHIPS):
            r2s[step, i] = summed[i * ROWS:(i + 1) * ROWS]
        r2_index = next(numbers)
        for c, device in zip(to_ids, chips):
            push(r2s.at[step, c], r2.at[step, chip], r2_index, device)
        r2[step, chip] = r2s[step, chip]
        r2_size = r2.at[step, pl.ds(0, CHIPS - 1)]
        used.append((r2_size, r2_index))
        wait_a1()
        a2[step, chip] = coupled + a1[step]
        wait_a2 = offer(a2.at[step], chip, chips)

        rv, rp = section_of(total, 2), section_of(total, 3)
        if step:
            block = block - dot(pv_spread[:ROWS, :ROWS], basis, precision=HIGHEST)
            crossed = dot(rv, pv_spread, nt=True, precision=HIGHEST)
            crossed_t = dot(pv, spread(rv, mask), nt=True, precision=HIGHEST)
            inner = dot(pv, spread(own_energy, mask), precision=HIGHEST)
            rp = rp - crossed - crossed_t + dot(inner, pv_spread, nt=True, precision=HIGHEST)
        basis = dot(inverse_spread[:ROWS, :ROWS], block, precision=HIGHEST)
        half = dot(inverse, spread(rp, mask), precision=HIGHEST)
        own_energy = dot(half, inverse_spread, nt=True, precision=HIGHEST)

        await_bytes(r2_size, recv, r2_index)
        r3[step, t] = add_up(r2.at[step], CHIPS).astype(BF16)
        wait_r3 = offer(r3.at[step], t, tiles)
        wait_a2()
        a3[step, t] = add_up(a2.at[step], CHIPS)
        wait_a3 = offer(a3.at[step], t, tiles)
        wait_r3()
        sigma = energy * basis + by_k_point(add_up(r3.at[step], TILE), False)
        wait_a3()
        ray_t = fold(add_up(a3.at[step], TILE)) * (1.0 / count) + own_energy
        residual = sigma - dot(spread(ray_t, mask)[:ROWS, :ROWS], basis, precision=HIGHEST)
        block = residual / energy
        sums = grams(
            jnp.concatenate([block, residual], 0), jnp.concatenate([basis, block], 0)
        )
        eye = (iota((NV, SPAN), 0) == iota((NV, SPAN), 1)).astype(F32)
        first = jnp.where(iota((NV, SPAN), 1) < NV, ray_t, 0.0)
        ray_ref[step] = dot(eye, first, nt=True, precision=HIGHEST)

    f1[t] = sums
    wait_f1 = offer(f1, t, tiles)
    res_ref[...] = residual
    wait_f1()
    f2[core, chip] = add_up(f1, TILE)
    offer(f2.at[core], chip, chips)()
    hand(f2.at[core], f2.at[core])()
    total = jnp.zeros((NV, SPAN), F32)
    for i in range(CHIPS):
        for c in range(CORES):
            total = total + f2[c, i]
    pv, pp = section_of(total, 0), section_of(total, 1)
    pv_spread = spread(pv, mask)
    gram = pp - dot(pv, pv_spread, nt=True, precision=HIGHEST)
    inverse_spread = spread(factor(gram)[0], mask)
    block = block - dot(pv_spread[:ROWS, :ROWS], basis, precision=HIGHEST)
    basis_ref[...] = dot(inverse_spread[:ROWS, :ROWS], block, precision=HIGHEST)

    for ref, index in used:
        await_bytes(ref, send, index)


def hand_out(ray, basis, residual, ray_out, basis_out, residual_out):
    basis_out[...] = basis[...]
    residual_out[...] = residual[...]
    ray_out[...] = ray[...]


def per_device(coeff, energy, ranks, assign, screen, initial):
    width = initial.shape[2]
    count = initial.shape[0] * GRP * width * TILE
    vmem = pl.BlockSpec(memory_space=pltpu.VMEM)
    hbm = pl.BlockSpec(memory_space=pltpu.HBM)
    ray, basis, residual = pl.pallas_call(
        functools.partial(body, count),
        out_shape=[
            jax.ShapeDtypeStruct((ITERS, NV, NV), F32),
            jax.ShapeDtypeStruct((ROWS, width), F32),
            jax.ShapeDtypeStruct((ROWS, width), F32),
        ],
        in_specs=[hbm] * 6,
        out_specs=[vmem, vmem, vmem],
        scratch_shapes=[
            pltpu.VMEM(coeff.shape, BF16),
            pltpu.VMEM(screen.shape, BF16),
            pltpu.VMEM((ITERS, TILE, NV, SPAN), F32),
            pltpu.VMEM((ITERS, CORES, CHIPS, NV, SPAN), F32),
            pltpu.VMEM((ITERS, CORES, CHIPS, NV, SPAN), F32),
            pltpu.VMEM((ITERS, TILE, ROWS, LEV), F32),
            pltpu.VMEM((ITERS, CORES, CHIPS, ROWS, LEV), BF16),
            pltpu.VMEM((ALL, LEV), F32),
            pltpu.VMEM((ALL, LEV), BF16),
            pltpu.VMEM((ALL // 2, LEV), F32),
            pltpu.VMEM((ALL, ALL // 2), BF16),
            pltpu.VMEM((ALL // 2, ALL), BF16),
            pltpu.VMEM((ALL // 2, LEV), F32),
            pltpu.VMEM((ITERS, ALL // 2, LEV), BF16),
            pltpu.VMEM((ITERS, ALL // 2, LEV), BF16),
            pltpu.VMEM((ITERS, NV, SPAN), F32),
            pltpu.VMEM((ITERS, NV, SPAN), F32),
            pltpu.VMEM((ITERS, CHIPS, ROWS, LEV), BF16),
            pltpu.VMEM((ITERS, CHIPS, ROWS, LEV), BF16),
            pltpu.VMEM((ITERS, CHIPS, NV, SPAN), F32),
            pltpu.VMEM((ITERS, TILE, ROWS, LEV), BF16),
            pltpu.VMEM((ITERS, TILE, NV, SPAN), F32),
            pltpu.VMEM((TILE, NV, SPAN), F32),
            pltpu.VMEM((CORES, CHIPS, NV, SPAN), F32),
            pltpu.SMEM(assign.shape, jnp.int32),
            pltpu.VMEM(ranks.shape, jnp.int32),
            pltpu.VMEM(energy.shape, F32),
            pltpu.VMEM((ROWS, width), F32),
            pltpu.SemaphoreType.DMA((6,)),
            pltpu.SemaphoreType.DMA((SEMS,)),
            pltpu.SemaphoreType.DMA((SEMS,)),
        ],
        compiler_params=pltpu.CompilerParams(
            collective_id=0, has_side_effects=True, vmem_limit_bytes=32 * 2**20
        ),
        name="davidson",
    )(*[pltpu.with_memory_space_constraint(a, pltpu.HBM) for a in (assign, ranks, coeff, screen, energy, initial.reshape(ROWS, width))])
    basis, residual = basis.reshape(initial.shape), residual.reshape(initial.shape)
    results = (ray, basis, residual)
    return tuple(pl.pallas_call(
        hand_out,
        out_shape=[jax.ShapeDtypeStruct(r.shape, r.dtype) for r in results],
        in_specs=[vmem] * 3,
        out_specs=[vmem] * 3,
        compiler_params=pltpu.CompilerParams(vmem_limit_bytes=8 * 2**20),
        name="hand_out",
    )(*results))


def solution(mesh):
    placed = (
        P("grp", None, "tile"),
        P("grp", "tile"),
        P(),
        P(("grp", "tile")),
        P(("grp", "tile"), None, None),
        P("grp", None, "tile"),
    )
    return jax.shard_map(
        per_device,
        mesh=mesh,
        in_specs=placed,
        out_specs=(P(), P("grp", None, "tile"), P("grp", None, "tile")),
        check_vma=False,
    )
```

```python
import functools

import jax
import jax.numpy as jnp
from jax import lax
from jax.experimental import pallas as pl
from jax.experimental.pallas import tpu as pltpu
from jax.sharding import PartitionSpec as P

ITERS = 2
NV = 8
GRP, TILE, CHIPS, CORES = 16, 8, 8, 2
LK = 4
ROWS = LK * NV
ALL = GRP * ROWS
LEV = 256
TASKS = 32
SEMS = 64
SPAN = 128
F32, BF16 = jnp.float32, jnp.bfloat16
HIGHEST = lax.Precision.HIGHEST
MESH = pl.DeviceIdType.MESH
CHIP_STEPS = ((1, 2), (0, 2), (1, 1), (1, 3), (0, 1), (0, 3), (1, 0))
TILE_STEPS = ((1, 2), (1, 1), (1, 3), (1, 0), (0, 2), (0, 1), (0, 3))


def dot(a, b, nt=False, precision=None):
    return lax.dot_general(
        a, b, (((1,), (1 if nt else 0,)), ((), ())),
        precision=precision, preferred_element_type=F32,
    )


def split(a):
    high = a.astype(BF16)
    return high, (a - high.astype(F32)).astype(BF16)


def iota(shape, dim):
    return lax.broadcasted_iota(jnp.int32, shape, dim)


def block_mask(rows, cols):
    return (iota((rows, cols), 0) // NV) == (iota((rows, cols), 1) // NV)


def fold(part):
    for step in (8, 16, 32, 64):
        part = part + pltpu.roll(part, step, 1)
    return part


def sum_groups(a):
    total = a[0:NV]
    for i in range(1, a.shape[0] // NV):
        total = total + a[i * NV:(i + 1) * NV]
    return total


def spread(small, mask):
    return jnp.where(mask, jnp.concatenate([small] * (SPAN // NV), axis=0), 0.0)


def factor(gram, ridge=False):
    whole = (NV, SPAN)
    columns = [jnp.broadcast_to(gram[:, m:m + 1], whole) for m in range(NV)]
    e = [[jnp.broadcast_to(columns[m][n:n + 1, :], whole) for m in range(n + 1)] for n in range(NV)]
    if ridge:
        trace = e[0][0]
        for n in range(1, NV):
            trace = trace + e[n][n]
        for n in range(NV):
            e[n][n] = e[n][n] + (trace * 1e-6 + 1e-30)
    unit = [[None] * NV for _ in range(NV)]
    for j in range(NV):
        inverse_pivot = 1.0 / e[j][j]
        for i in range(j + 1, NV):
            unit[i][j] = e[i][j] * inverse_pivot
            for m in range(j + 1, i + 1):
                e[i][m] = e[i][m] - unit[i][j] * e[m][j]
    back = [[None] * NV for _ in range(NV)]
    for j in range(NV):
        for i in range(j + 1, NV):
            value = unit[i][j]
            for q in range(j + 1, i):
                value = value + unit[i][q] * back[q][j]
            back[i][j] = -value
    scale = [lax.rsqrt(e[n][n]) for n in range(NV)]
    root = [e[n][n] * scale[n] for n in range(NV)]
    sub, lane = iota(whole, 0), iota(whole, 1) % NV

    def assemble(entry):
        out = jnp.zeros(whole, F32)
        for i in range(NV):
            row = jnp.zeros(whole, F32)
            for j in range(i + 1):
                row = jnp.where(lane == j, entry(i, j), row)
            out = jnp.where(sub == i, row, out)
        return out

    inverse = assemble(lambda i, j: scale[i] if i == j else scale[i] * back[i][j])
    lower = assemble(lambda i, j: root[i] if i == j else unit[i][j] * root[j])
    return inverse, lower


def body(
    count, assign_hbm, ranks_hbm, coeff_hbm, screen_hbm, energy_hbm, x_hbm,
    ray_ref, basis_ref, res_ref,
    coeff, screen, g1, g2, t2, d1, d2, dens, dens_b, term, before, e8, pick, pick_group, keep,
    r1s, r1, a1s, a1, r2s, r2, a2, r3, a3, f1, f2,
    assign_ref, ranks_ref, energy_ref, x_ref, load_sem, send, recv,
):
    g, t = lax.axis_index("grp"), lax.axis_index("tile")
    core, chip = lax.rem(g, CORES), lax.div(g, CORES)
    y_lo, x = lax.div(chip, 4), lax.rem(chip, 4)
    y_hi, z = lax.div(t, 4), lax.rem(t, 4)
    sibling = (chip * CORES + (1 - core), t)
    to_ids = [lax.rem(y_lo + a, 2) * 4 + lax.rem(x + b, 4) for a, b in CHIP_STEPS]
    from_ids = [lax.rem(y_lo + 2 - a, 2) * 4 + lax.rem(x + 4 - b, 4) for a, b in CHIP_STEPS]
    chips = [(c * CORES + core, t) for c in to_ids]
    tiles = [(g, lax.rem(y_hi + a, 2) * 4 + lax.rem(z + b, 4)) for a, b in TILE_STEPS]

    half_rows = ALL // 2
    barrier = pltpu.get_barrier_semaphore()
    peers = [*tiles, *chips, sibling]
    for peer in peers:
        pl.semaphore_signal(barrier, inc=1, device_id=peer, device_id_type=MESH)
    loads = [
        pltpu.make_async_copy(src, dst, load_sem.at[i])
        for i, (src, dst) in enumerate((
            (x_hbm, x_ref), (energy_hbm, energy_ref), (coeff_hbm, coeff),
            (assign_hbm, assign_ref), (ranks_hbm, ranks_ref), (screen_hbm, screen),
        ))
    ]
    for load in loads:
        load.start()

    used = []
    numbers = iter(range(SEMS))

    def push(src, dst, index, device):
        pltpu.make_async_remote_copy(
            src_ref=src, dst_ref=dst, send_sem=send.at[index], recv_sem=recv.at[index],
            device_id=device, device_id_type=MESH,
        ).start()

    def await_bytes(ref, sems, index):
        pltpu.make_async_copy(ref, ref, sems.at[index]).wait()

    def offer(buf, mine, devices):
        index = next(numbers)
        for device in devices:
            push(buf.at[mine], buf.at[mine], index, device)
        size = buf.at[pl.ds(0, len(devices))]
        used.append((size, index))
        return lambda: await_bytes(size, recv, index)

    def hand(src, dst):
        index = next(numbers)
        push(src, dst, index, sibling)
        used.append((dst, index))
        return lambda: await_bytes(dst, recv, index)

    def add_up(buf, n):
        total = buf[0].astype(F32)
        for i in range(1, n):
            total = total + buf[i].astype(F32)
        return total

    mask = block_mask(SPAN, SPAN)
    mask_gram = ((iota((2 * ROWS, 2 * ROWS), 0) % ROWS) // NV) == (
        (iota((2 * ROWS, 2 * ROWS), 1) % ROWS) // NV
    )
    section = iota((NV, SPAN), 1) // ROWS

    def grams(left, right):
        full = jnp.where(mask_gram, dot(left, right, nt=True, precision=HIGHEST), 0.0)
        return jnp.concatenate([sum_groups(full[:ROWS]), sum_groups(full[ROWS:])], axis=1)

    def by_k_point(block, nt):
        low = block - block.astype(BF16).astype(F32)
        out = []
        for k in range(LK):
            rows = slice(k * NV, (k + 1) * NV)
            both = jnp.concatenate([block[rows], low[rows]], axis=0).astype(BF16)
            got = dot(both, coeff[k], nt=nt)
            out.append(got[:NV] + got[NV:])
        return jnp.concatenate(out, axis=0)

    def section_of(total, which):
        return fold(jnp.where(section == which, total, 0.0)) * (1.0 / count)

    def place(k):
        return ((k >> 2) & 1) * half_rows + (k >> 3) * ROWS + (k & 3) * NV

    def one_hots():
        for load in loads[3:5]:
            load.wait()
        lane_task = iota((1, half_rows), 1) // NV
        target = jnp.zeros((1, half_rows), jnp.int32)
        pairs = []
        for i in range(TASKS):
            pair = assign_ref[i]
            target = jnp.where(lane_task == i, place(pair >> 6), target)
            pairs.append(jnp.full((NV, SPAN), pair, jnp.int32))
        target = target + iota((1, half_rows), 1) % NV
        e8[...] = (iota((ALL, half_rows), 0) == target).astype(F32).astype(BF16)
        pairs = jnp.concatenate(pairs, axis=0)
        task_row, task_col = pairs >> 6, pairs & 63
        lane = iota((half_rows, SPAN), 1)
        source_row = place(task_col) + iota((half_rows, SPAN), 0) % NV
        for j in range(ALL // SPAN):
            pick[:, j * SPAN:(j + 1) * SPAN] = (
                (lane + j * SPAN == source_row).astype(F32).astype(BF16)
            )
        group_row = (place(task_col) // ROWS) * NV + iota((half_rows, SPAN), 0) % NV
        pick_group[...] = (lane == group_row).astype(F32).astype(BF16)
        k_points = GRP * LK
        chosen = dot((lane[:, :k_points] == task_row[:, :k_points]).astype(F32).astype(BF16),
                     ranks_ref[...].astype(F32).astype(BF16))
        chosen = jnp.where(lane[:, :k_points] == task_col[:, :k_points], chosen, 0.0)
        rank = jnp.sum(chosen, axis=1, keepdims=True)
        keep[...] = (iota((half_rows, LEV), 1).astype(F32) < rank).astype(F32)

    def apply(high, low, rows):
        rows_high, rows_low = split(rows)
        return (
            dot(jnp.concatenate([high, high], axis=1), jnp.concatenate([rows_high, rows_low], axis=0))
            + dot(low, rows_high)
        )

    for load in loads[:2]:
        load.wait()
    energy = jnp.concatenate(
        [jnp.broadcast_to(energy_ref[k:k + 1, :], (NV, energy_ref.shape[1])) for k in range(LK)],
        axis=0,
    )
    block = x_ref[...]
    zeros = jnp.zeros_like(block)
    sums = grams(jnp.concatenate([block, energy * block], 0), jnp.concatenate([zeros, block], 0))
    loads[2].wait()
    payload = by_k_point(block, True)
    pl.semaphore_wait(barrier, len(peers))

    basis = None
    own_energy = None
    residual = None
    mine = pl.ds(pl.multiple_of(core * half_rows, half_rows), half_rows)
    theirs = pl.ds(pl.multiple_of((1 - core) * half_rows, half_rows), half_rows)
    for step in range(ITERS):
        g1[step, t] = sums
        wait_g1 = offer(g1.at[step], t, tiles)
        if step:
            payload = by_k_point(block, True)
        d1[step, t] = payload
        wait_d1 = offer(d1.at[step], t, tiles)
        if step == 0:
            one_hots()
        wait_g1()
        total = add_up(g1.at[step], TILE)
        g2[step, core, chip] = total
        wait_g2 = offer(g2.at[step, core], chip, chips)
        own_inverse, own_factor = factor(section_of(total, 1), ridge=True)
        t2[step, core, chip] = own_factor
        wait_t2 = offer(t2.at[step, core], chip, chips)
        own_inverse = spread(own_inverse, mask)[:ROWS, :ROWS]
        wait_d1()
        total = add_up(d1.at[step], TILE)
        d2[step, core, chip] = dot(own_inverse, total, precision=HIGHEST).astype(BF16)
        mine_now = d2.at[step, core, chip]
        arrivals = [next(numbers) for _ in chips]
        for index, device in zip(arrivals, chips):
            push(mine_now, mine_now, index, device)
            used.append((mine_now, index))
        pass_on = next(numbers)
        push(mine_now, mine_now, pass_on, sibling)
        wait_g2()
        wait_h2 = hand(g2.at[step, core], g2.at[step, core])
        wait_t2()
        wait_u2 = hand(t2.at[step, core], t2.at[step, core])
        for index, source in reversed(list(zip(arrivals, from_ids))):
            landed = d2.at[step, core, source]
            await_bytes(landed, recv, index)
            push(landed, landed, pass_on, sibling)
        wait_h2()
        wait_u2()
        whole = d2.at[step, 0]
        used.append((whole, pass_on))
        await_bytes(whole, recv, pass_on)
        if step == 0:
            loads[5].wait()
        chosen = dot(pick[...], d2[step].reshape(ALL, LEV)) * keep[...]
        for i in range(TASKS):
            rows = slice(i * NV, (i + 1) * NV)
            term[rows, :] = dot(chosen[rows].astype(BF16), screen[i], nt=True)

        total = jnp.zeros((NV, SPAN), F32)
        for i in range(CHIPS):
            for c in range(CORES):
                total = total + g2[step, c, i]
        pv, pp = section_of(total, 0), section_of(total, 1)
        pv_spread = spread(pv, mask)
        gram = pp
        if step:
            gram = pp - dot(pv, pv_spread, nt=True, precision=HIGHEST)
        inverse, _ = factor(gram)
        inverse_spread = spread(inverse, mask)
        columns = [jnp.broadcast_to(inverse[:, m:m + 1], (NV, SPAN)) for m in range(NV)]
        mixed_t = []
        for j in range(GRP):
            theirs_t = t2[step, j // CHIPS, j % CHIPS]
            mixed = columns[0] * theirs_t[0:1, :]
            for m in range(1, NV):
                mixed = mixed + columns[m] * theirs_t[m:m + 1, :]
            mixed_t.append(mixed)
        group_high, group_low = split(jnp.concatenate(mixed_t, axis=0))
        if step:
            old = dot(inverse, pv_spread, precision=HIGHEST)
            old_high, old_low = split(spread(old, mask))
        terms = []
        for j in range(half_rows // SPAN):
            rows = slice(j * SPAN, (j + 1) * SPAN)
            high = jnp.where(mask, dot(pick_group[rows, :], group_high), 0.0).astype(BF16)
            low = jnp.where(mask, dot(pick_group[rows, :], group_low), 0.0).astype(BF16)
            result = apply(high, low, term[rows, :])
            if step:
                result = result - apply(old_high, old_low, before[rows, :])
            if step + 1 < ITERS:
                before[rows, :] = result
            terms.append(result)
        term_high, term_low = split(jnp.concatenate(terms, axis=0) * keep[...])

        r1s[step] = (dot(e8[theirs, :], term_high) + dot(e8[theirs, :], term_low)).astype(BF16)
        wait_r1 = hand(r1s.at[step], r1.at[step])
        for j in range(ALL // SPAN):
            rows = slice(j * SPAN, (j + 1) * SPAN)
            parts = [mixed_t[j * 4 + i] for i in range(4) for _ in range(LK)]
            high, low = split(jnp.where(mask, jnp.concatenate(parts, axis=0), 0.0))
            landed = d2[step, j // 2, (j % 2) * 4:(j % 2) * 4 + 4].reshape(SPAN, LEV)
            mixed = dot(high, landed) + dot(low, landed)
            if step:
                mixed = mixed - apply(old_high, old_low, dens[rows, :])
            dens_b[rows, :] = mixed.astype(BF16)
            if step + 1 < ITERS:
                dens[rows, :] = mixed
        own = dot(e8[mine, :], term_high) + dot(e8[mine, :], term_low)
        own_b = own.astype(BF16)
        coupled = jnp.zeros((SPAN, SPAN), F32)
        for j in range(half_rows // SPAN):
            rows = slice(j * SPAN, (j + 1) * SPAN)
            coupled = coupled + dot(r1s[step, rows, :], dens_b[theirs, :][rows], nt=True)
            coupled = coupled + dot(own_b[rows], dens_b[mine, :][rows], nt=True)
        coupled = sum_groups(jnp.where(mask, coupled, 0.0))
        a1s[step] = coupled
        wait_a1 = hand(a1s.at[step], a1.at[step])
        wait_r1()
        summed = (own + r1[step].astype(F32)).astype(BF16)
        for i in range(CHIPS):
            r2s[step, i] = summed[i * ROWS:(i + 1) * ROWS]
        r2_index = next(numbers)
        for c, device in zip(to_ids, chips):
            push(r2s.at[step, c], r2.at[step, chip], r2_index, device)
        r2[step, chip] = r2s[step, chip]
        r2_size = r2.at[step, pl.ds(0, CHIPS - 1)]
        used.append((r2_size, r2_index))
        wait_a1()
        a2[step, chip] = coupled + a1[step]
        wait_a2 = offer(a2.at[step], chip, chips)

        rv, rp = section_of(total, 2), section_of(total, 3)
        if step:
            block = block - dot(pv_spread[:ROWS, :ROWS], basis, precision=HIGHEST)
            crossed = dot(rv, pv_spread, nt=True, precision=HIGHEST)
            crossed_t = dot(pv, spread(rv, mask), nt=True, precision=HIGHEST)
            inner = dot(pv, spread(own_energy, mask), precision=HIGHEST)
            rp = rp - crossed - crossed_t + dot(inner, pv_spread, nt=True, precision=HIGHEST)
        basis = dot(inverse_spread[:ROWS, :ROWS], block, precision=HIGHEST)
        half = dot(inverse, spread(rp, mask), precision=HIGHEST)
        own_energy = dot(half, inverse_spread, nt=True, precision=HIGHEST)

        await_bytes(r2_size, recv, r2_index)
        r3[step, t] = add_up(r2.at[step], CHIPS).astype(BF16)
        wait_r3 = offer(r3.at[step], t, tiles)
        wait_a2()
        a3[step, t] = add_up(a2.at[step], CHIPS)
        wait_a3 = offer(a3.at[step], t, tiles)
        wait_r3()
        sigma = energy * basis + by_k_point(add_up(r3.at[step], TILE), False)
        wait_a3()
        ray_t = fold(add_up(a3.at[step], TILE)) * (1.0 / count) + own_energy
        residual = sigma - dot(spread(ray_t, mask)[:ROWS, :ROWS], basis, precision=HIGHEST)
        block = residual / energy
        sums = grams(
            jnp.concatenate([block, residual], 0), jnp.concatenate([basis, block], 0)
        )
        eye = (iota((NV, SPAN), 0) == iota((NV, SPAN), 1)).astype(F32)
        first = jnp.where(iota((NV, SPAN), 1) < NV, ray_t, 0.0)
        ray_ref[step] = dot(eye, first, nt=True, precision=HIGHEST)

    f1[t] = sums
    wait_f1 = offer(f1, t, tiles)
    res_ref[...] = residual
    wait_f1()
    f2[core, chip] = add_up(f1, TILE)
    offer(f2.at[core], chip, chips)()
    hand(f2.at[core], f2.at[core])()
    total = jnp.zeros((NV, SPAN), F32)
    for i in range(CHIPS):
        for c in range(CORES):
            total = total + f2[c, i]
    pv, pp = section_of(total, 0), section_of(total, 1)
    pv_spread = spread(pv, mask)
    gram = pp - dot(pv, pv_spread, nt=True, precision=HIGHEST)
    inverse_spread = spread(factor(gram)[0], mask)
    block = block - dot(pv_spread[:ROWS, :ROWS], basis, precision=HIGHEST)
    basis_ref[...] = dot(inverse_spread[:ROWS, :ROWS], block, precision=HIGHEST)

    for ref, index in used:
        await_bytes(ref, send, index)


def hand_out(ray, basis, residual, ray_out, basis_out, residual_out):
    basis_out[...] = basis[...]
    residual_out[...] = residual[...]
    ray_out[...] = ray[...]


def per_device(coeff, energy, ranks, assign, screen, initial):
    width = initial.shape[2]
    count = initial.shape[0] * GRP * width * TILE
    vmem = pl.BlockSpec(memory_space=pltpu.VMEM)
    hbm = pl.BlockSpec(memory_space=pltpu.HBM)
    ray, basis, residual = pl.pallas_call(
        functools.partial(body, count),
        out_shape=[
            jax.ShapeDtypeStruct((ITERS, NV, NV), F32),
            jax.ShapeDtypeStruct((ROWS, width), F32),
            jax.ShapeDtypeStruct((ROWS, width), F32),
        ],
        in_specs=[hbm] * 6,
        out_specs=[vmem, vmem, vmem],
        scratch_shapes=[
            pltpu.VMEM(coeff.shape, BF16),
            pltpu.VMEM(screen.shape, BF16),
            pltpu.VMEM((ITERS, TILE, NV, SPAN), F32),
            pltpu.VMEM((ITERS, CORES, CHIPS, NV, SPAN), F32),
            pltpu.VMEM((ITERS, CORES, CHIPS, NV, SPAN), F32),
            pltpu.VMEM((ITERS, TILE, ROWS, LEV), F32),
            pltpu.VMEM((ITERS, CORES, CHIPS, ROWS, LEV), BF16),
            pltpu.VMEM((ALL, LEV), F32),
            pltpu.VMEM((ALL, LEV), BF16),
            pltpu.VMEM((ALL // 2, LEV), F32),
            pltpu.VMEM((ALL // 2, LEV), F32),
            pltpu.VMEM((ALL, ALL // 2), BF16),
            pltpu.VMEM((ALL // 2, ALL), BF16),
            pltpu.VMEM((ALL // 2, SPAN), BF16),
            pltpu.VMEM((ALL // 2, LEV), F32),
            pltpu.VMEM((ITERS, ALL // 2, LEV), BF16),
            pltpu.VMEM((ITERS, ALL // 2, LEV), BF16),
            pltpu.VMEM((ITERS, NV, SPAN), F32),
            pltpu.VMEM((ITERS, NV, SPAN), F32),
            pltpu.VMEM((ITERS, CHIPS, ROWS, LEV), BF16),
            pltpu.VMEM((ITERS, CHIPS, ROWS, LEV), BF16),
            pltpu.VMEM((ITERS, CHIPS, NV, SPAN), F32),
            pltpu.VMEM((ITERS, TILE, ROWS, LEV), BF16),
            pltpu.VMEM((ITERS, TILE, NV, SPAN), F32),
            pltpu.VMEM((TILE, NV, SPAN), F32),
            pltpu.VMEM((CORES, CHIPS, NV, SPAN), F32),
            pltpu.SMEM(assign.shape, jnp.int32),
            pltpu.VMEM(ranks.shape, jnp.int32),
            pltpu.VMEM(energy.shape, F32),
            pltpu.VMEM((ROWS, width), F32),
            pltpu.SemaphoreType.DMA((6,)),
            pltpu.SemaphoreType.DMA((SEMS,)),
            pltpu.SemaphoreType.DMA((SEMS,)),
        ],
        compiler_params=pltpu.CompilerParams(
            collective_id=0, has_side_effects=True, vmem_limit_bytes=32 * 2**20
        ),
        name="davidson",
    )(*[pltpu.with_memory_space_constraint(a, pltpu.HBM) for a in (assign, ranks, coeff, screen, energy, initial.reshape(ROWS, width))])
    basis, residual = basis.reshape(initial.shape), residual.reshape(initial.shape)
    results = (ray, basis, residual)
    return tuple(pl.pallas_call(
        hand_out,
        out_shape=[jax.ShapeDtypeStruct(r.shape, r.dtype) for r in results],
        in_specs=[vmem] * 3,
        out_specs=[vmem] * 3,
        compiler_params=pltpu.CompilerParams(vmem_limit_bytes=8 * 2**20),
        name="hand_out",
    )(*results))


def solution(mesh):
    placed = (
        P("grp", None, "tile"),
        P("grp", "tile"),
        P(),
        P(("grp", "tile")),
        P(("grp", "tile"), None, None),
        P("grp", None, "tile"),
    )
    return jax.shard_map(
        per_device,
        mesh=mesh,
        in_specs=placed,
        out_specs=(P(), P("grp", None, "tile"), P("grp", None, "tile")),
        check_vma=False,
    )
```

```python
import functools

import jax
import jax.numpy as jnp
from jax import lax
from jax.experimental import pallas as pl
from jax.experimental.pallas import tpu as pltpu
from jax.sharding import PartitionSpec as P

ITERS = 2
NV = 8
GRP, TILE, CHIPS, CORES = 16, 8, 8, 2
LK = 4
ROWS = LK * NV
ALL = GRP * ROWS
LEV = 256
TASKS = 32
SEMS = 64
SPAN = 128
F32, BF16 = jnp.float32, jnp.bfloat16
HIGHEST = lax.Precision.HIGHEST
MESH = pl.DeviceIdType.MESH
CHIP_STEPS = ((1, 2), (0, 2), (1, 1), (1, 3), (0, 1), (0, 3), (1, 0))
TILE_STEPS = ((1, 2), (1, 1), (1, 3), (1, 0), (0, 2), (0, 1), (0, 3))


def dot(a, b, nt=False, precision=None):
    return lax.dot_general(
        a, b, (((1,), (1 if nt else 0,)), ((), ())),
        precision=precision, preferred_element_type=F32,
    )


def split(a):
    high = a.astype(BF16)
    return high, (a - high.astype(F32)).astype(BF16)


def iota(shape, dim):
    return lax.broadcasted_iota(jnp.int32, shape, dim)


def block_mask(rows, cols):
    return (iota((rows, cols), 0) // NV) == (iota((rows, cols), 1) // NV)


def fold(part):
    for step in (8, 16, 32, 64):
        part = part + pltpu.roll(part, step, 1)
    return part


def sum_groups(a):
    total = a[0:NV]
    for i in range(1, a.shape[0] // NV):
        total = total + a[i * NV:(i + 1) * NV]
    return total


def spread(small, mask):
    return jnp.where(mask, jnp.concatenate([small] * (SPAN // NV), axis=0), 0.0)


def factor(gram, ridge=False):
    whole = (NV, SPAN)
    columns = [jnp.broadcast_to(gram[:, m:m + 1], whole) for m in range(NV)]
    e = [[jnp.broadcast_to(columns[m][n:n + 1, :], whole) for m in range(n + 1)] for n in range(NV)]
    if ridge:
        trace = e[0][0]
        for n in range(1, NV):
            trace = trace + e[n][n]
        for n in range(NV):
            e[n][n] = e[n][n] + (trace * 1e-6 + 1e-30)
    unit = [[None] * NV for _ in range(NV)]
    for j in range(NV):
        inverse_pivot = 1.0 / e[j][j]
        for i in range(j + 1, NV):
            unit[i][j] = e[i][j] * inverse_pivot
            for m in range(j + 1, i + 1):
                e[i][m] = e[i][m] - unit[i][j] * e[m][j]
    back = [[None] * NV for _ in range(NV)]
    for j in range(NV):
        for i in range(j + 1, NV):
            value = unit[i][j]
            for q in range(j + 1, i):
                value = value + unit[i][q] * back[q][j]
            back[i][j] = -value
    scale = [lax.rsqrt(e[n][n]) for n in range(NV)]
    root = [e[n][n] * scale[n] for n in range(NV)]
    sub, lane = iota(whole, 0), iota(whole, 1) % NV

    def assemble(entry):
        out = jnp.zeros(whole, F32)
        for i in range(NV):
            row = jnp.zeros(whole, F32)
            for j in range(i + 1):
                row = jnp.where(lane == j, entry(i, j), row)
            out = jnp.where(sub == i, row, out)
        return out

    inverse = assemble(lambda i, j: scale[i] if i == j else scale[i] * back[i][j])
    lower = assemble(lambda i, j: root[i] if i == j else unit[i][j] * root[j])
    return inverse, lower


def body(
    count, assign_hbm, ranks_hbm, coeff_hbm, screen_hbm, energy_hbm, x_hbm,
    ray_ref, basis_ref, res_ref,
    coeff, screen, g1, g2, t2, d1, d2, dens, dens_b, term, before, e8, pick, pick_group, keep,
    r1s, r1, a1s, a1, r2s, r2, a2, r3, a3, f1, f2,
    assign_ref, ranks_ref, energy_ref, x_ref, load_sem, send, recv,
):
    g, t = lax.axis_index("grp"), lax.axis_index("tile")
    core, chip = lax.rem(g, CORES), lax.div(g, CORES)
    y_lo, x = lax.div(chip, 4), lax.rem(chip, 4)
    y_hi, z = lax.div(t, 4), lax.rem(t, 4)
    sibling = (chip * CORES + (1 - core), t)
    to_ids = [lax.rem(y_lo + a, 2) * 4 + lax.rem(x + b, 4) for a, b in CHIP_STEPS]
    from_ids = [lax.rem(y_lo + 2 - a, 2) * 4 + lax.rem(x + 4 - b, 4) for a, b in CHIP_STEPS]
    chips = [(c * CORES + core, t) for c in to_ids]
    tiles = [(g, lax.rem(y_hi + a, 2) * 4 + lax.rem(z + b, 4)) for a, b in TILE_STEPS]

    half_rows = ALL // 2
    barrier = pltpu.get_barrier_semaphore()
    peers = [*tiles, *chips, sibling]
    for peer in peers:
        pl.semaphore_signal(barrier, inc=1, device_id=peer, device_id_type=MESH)
    loads = [
        pltpu.make_async_copy(src, dst, load_sem.at[i])
        for i, (src, dst) in enumerate((
            (x_hbm, x_ref), (energy_hbm, energy_ref), (coeff_hbm, coeff),
            (assign_hbm, assign_ref), (ranks_hbm, ranks_ref), (screen_hbm, screen),
        ))
    ]
    for load in loads:
        load.start()

    used = []
    numbers = iter(range(SEMS))

    def push(src, dst, index, device):
        pltpu.make_async_remote_copy(
            src_ref=src, dst_ref=dst, send_sem=send.at[index], recv_sem=recv.at[index],
            device_id=device, device_id_type=MESH,
        ).start()

    def await_bytes(ref, sems, index):
        pltpu.make_async_copy(ref, ref, sems.at[index]).wait()

    def offer(buf, mine, devices):
        index = next(numbers)
        for device in devices:
            push(buf.at[mine], buf.at[mine], index, device)
        size = buf.at[pl.ds(0, len(devices))]
        used.append((size, index))
        return lambda: await_bytes(size, recv, index)

    def hand(src, dst):
        index = next(numbers)
        push(src, dst, index, sibling)
        used.append((dst, index))
        return lambda: await_bytes(dst, recv, index)

    def add_up(buf, n):
        total = buf[0].astype(F32)
        for i in range(1, n):
            total = total + buf[i].astype(F32)
        return total

    mask = block_mask(SPAN, SPAN)
    mask_gram = ((iota((2 * ROWS, 2 * ROWS), 0) % ROWS) // NV) == (
        (iota((2 * ROWS, 2 * ROWS), 1) % ROWS) // NV
    )
    section = iota((NV, SPAN), 1) // ROWS

    def grams(left, right):
        full = jnp.where(mask_gram, dot(left, right, nt=True, precision=HIGHEST), 0.0)
        return jnp.concatenate([sum_groups(full[:ROWS]), sum_groups(full[ROWS:])], axis=1)

    def by_k_point(block, nt):
        low = block - block.astype(BF16).astype(F32)
        out = []
        for k in range(LK):
            rows = slice(k * NV, (k + 1) * NV)
            both = jnp.concatenate([block[rows], low[rows]], axis=0).astype(BF16)
            got = dot(both, coeff[k], nt=nt)
            out.append(got[:NV] + got[NV:])
        return jnp.concatenate(out, axis=0)

    def section_of(total, which):
        return fold(jnp.where(section == which, total, 0.0)) * (1.0 / count)

    def place(k):
        return ((k >> 2) & 1) * half_rows + (k >> 3) * ROWS + (k & 3) * NV

    def one_hots():
        for load in loads[3:5]:
            load.wait()
        lane_task = iota((1, half_rows), 1) // NV
        target = jnp.zeros((1, half_rows), jnp.int32)
        pairs = []
        for i in range(TASKS):
            pair = assign_ref[i]
            target = jnp.where(lane_task == i, place(pair >> 6), target)
            pairs.append(jnp.full((NV, SPAN), pair, jnp.int32))
        target = target + iota((1, half_rows), 1) % NV
        e8[...] = (iota((ALL, half_rows), 0) == target).astype(F32).astype(BF16)
        pairs = jnp.concatenate(pairs, axis=0)
        task_row, task_col = pairs >> 6, pairs & 63
        lane = iota((half_rows, SPAN), 1)
        source_row = place(task_col) + iota((half_rows, SPAN), 0) % NV
        for j in range(ALL // SPAN):
            pick[:, j * SPAN:(j + 1) * SPAN] = (
                (lane + j * SPAN == source_row).astype(F32).astype(BF16)
            )
        group_row = (place(task_col) // ROWS) * NV + iota((half_rows, SPAN), 0) % NV
        pick_group[...] = (lane == group_row).astype(F32).astype(BF16)
        k_points = GRP * LK
        chosen = dot((lane[:, :k_points] == task_row[:, :k_points]).astype(F32).astype(BF16),
                     ranks_ref[...].astype(F32).astype(BF16))
        chosen = jnp.where(lane[:, :k_points] == task_col[:, :k_points], chosen, 0.0)
        rank = jnp.sum(chosen, axis=1, keepdims=True)
        keep[...] = (iota((half_rows, LEV), 1).astype(F32) < rank).astype(F32)

    def apply(high, low, rows):
        rows_high, rows_low = split(rows)
        return (
            dot(jnp.concatenate([high, high], axis=1), jnp.concatenate([rows_high, rows_low], axis=0))
            + dot(low, rows_high)
        )

    for load in loads[:2]:
        load.wait()
    energy = jnp.concatenate(
        [jnp.broadcast_to(energy_ref[k:k + 1, :], (NV, energy_ref.shape[1])) for k in range(LK)],
        axis=0,
    )
    block = x_ref[...]
    zeros = jnp.zeros_like(block)
    sums = grams(jnp.concatenate([block, energy * block], 0), jnp.concatenate([zeros, block], 0))
    loads[2].wait()
    payload = by_k_point(block, True)
    pl.semaphore_wait(barrier, len(peers))

    basis = None
    own_energy = None
    residual = None
    mine = pl.ds(pl.multiple_of(core * half_rows, half_rows), half_rows)
    theirs = pl.ds(pl.multiple_of((1 - core) * half_rows, half_rows), half_rows)
    for step in range(ITERS):
        g1[step, t] = sums
        wait_g1 = offer(g1.at[step], t, tiles)
        if step:
            payload = by_k_point(block, True)
        d1[step, t] = payload
        wait_d1 = offer(d1.at[step], t, tiles)
        if step == 0:
            one_hots()
        wait_g1()
        total = add_up(g1.at[step], TILE)
        g2[step, core, chip] = total
        wait_g2 = offer(g2.at[step, core], chip, chips)
        own_inverse, own_factor = factor(section_of(total, 1), ridge=True)
        t2[step, core, chip] = own_factor
        wait_t2 = offer(t2.at[step, core], chip, chips)
        own_inverse = spread(own_inverse, mask)[:ROWS, :ROWS]
        wait_d1()
        total = add_up(d1.at[step], TILE)
        d2[step, core, chip] = dot(own_inverse, total, precision=HIGHEST).astype(BF16)
        mine_now = d2.at[step, core, chip]
        arrivals = [next(numbers) for _ in chips]
        for index, device in zip(arrivals, chips):
            push(mine_now, mine_now, index, device)
            used.append((mine_now, index))
        pass_on = next(numbers)
        push(mine_now, mine_now, pass_on, sibling)
        wait_g2()
        wait_h2 = hand(g2.at[step, core], g2.at[step, core])
        wait_t2()
        wait_u2 = hand(t2.at[step, core], t2.at[step, core])
        for index, source in reversed(list(zip(arrivals, from_ids))):
            landed = d2.at[step, core, source]
            await_bytes(landed, recv, index)
            push(landed, landed, pass_on, sibling)
        wait_h2()
        wait_u2()
        whole = d2.at[step, 0]
        used.append((whole, pass_on))
        await_bytes(whole, recv, pass_on)
        if step == 0:
            loads[5].wait()
        chosen = dot(pick[...], d2[step].reshape(ALL, LEV)) * keep[...]
        for i in range(TASKS):
            rows = slice(i * NV, (i + 1) * NV)
            term[rows, :] = dot(chosen[rows].astype(BF16), screen[i], nt=True)

        total = jnp.zeros((NV, SPAN), F32)
        for i in range(CHIPS):
            for c in range(CORES):
                total = total + g2[step, c, i]
        pv, pp = section_of(total, 0), section_of(total, 1)
        pv_spread = spread(pv, mask)
        gram = pp
        if step:
            gram = pp - dot(pv, pv_spread, nt=True, precision=HIGHEST)
        inverse, _ = factor(gram)
        inverse_spread = spread(inverse, mask)
        columns = [jnp.broadcast_to(inverse[:, m:m + 1], (NV, SPAN)) for m in range(NV)]
        mixed_t = []
        for j in range(GRP):
            theirs_t = t2[step, j // CHIPS, j % CHIPS]
            mixed = columns[0] * theirs_t[0:1, :]
            for m in range(1, NV):
                mixed = mixed + columns[m] * theirs_t[m:m + 1, :]
            mixed_t.append(mixed)
        group_high, group_low = split(jnp.concatenate(mixed_t, axis=0))
        if step:
            old = dot(inverse, pv_spread, precision=HIGHEST)
            old_high, old_low = split(spread(old, mask))
        terms = []
        for j in range(half_rows // SPAN):
            rows = slice(j * SPAN, (j + 1) * SPAN)
            high = jnp.where(mask, dot(pick_group[rows, :], group_high), 0.0).astype(BF16)
            low = jnp.where(mask, dot(pick_group[rows, :], group_low), 0.0).astype(BF16)
            result = apply(high, low, term[rows, :])
            if step:
                result = result - apply(old_high, old_low, before[rows, :])
            if step + 1 < ITERS:
                before[rows, :] = result
            terms.append(result)
        term_high, term_low = split(jnp.concatenate(terms, axis=0) * keep[...])

        r1s[step] = (dot(e8[theirs, :], term_high) + dot(e8[theirs, :], term_low)).astype(BF16)
        wait_r1 = hand(r1s.at[step], r1.at[step])
        for j in range(ALL // SPAN):
            rows = slice(j * SPAN, (j + 1) * SPAN)
            parts = [mixed_t[j * 4 + i] for i in range(4) for _ in range(LK)]
            high, low = split(jnp.where(mask, jnp.concatenate(parts, axis=0), 0.0))
            landed = d2[step, j // 2, (j % 2) * 4:(j % 2) * 4 + 4].reshape(SPAN, LEV)
            mixed = dot(high, landed) + dot(low, landed)
            if step:
                mixed = mixed - apply(old_high, old_low, dens[rows, :])
            dens_b[rows, :] = mixed.astype(BF16)
            if step + 1 < ITERS:
                dens[rows, :] = mixed
        own = dot(e8[mine, :], term_high) + dot(e8[mine, :], term_low)
        own_b = own.astype(BF16)
        coupled = jnp.zeros((SPAN, SPAN), F32)
        for j in range(half_rows // SPAN):
            rows = slice(j * SPAN, (j + 1) * SPAN)
            coupled = coupled + dot(r1s[step, rows, :], dens_b[theirs, :][rows], nt=True)
            coupled = coupled + dot(own_b[rows], dens_b[mine, :][rows], nt=True)
        coupled = sum_groups(jnp.where(mask, coupled, 0.0))
        a1s[step] = coupled
        wait_a1 = hand(a1s.at[step], a1.at[step])
        wait_r1()
        summed = (own + r1[step].astype(F32)).astype(BF16)
        for i in range(CHIPS):
            r2s[step, i] = summed[i * ROWS:(i + 1) * ROWS]
        r2_index = next(numbers)
        for c, device in zip(to_ids, chips):
            push(r2s.at[step, c], r2.at[step, chip], r2_index, device)
        r2[step, chip] = r2s[step, chip]
        r2_size = r2.at[step, pl.ds(0, CHIPS - 1)]
        used.append((r2_size, r2_index))
        wait_a1()
        a2[step, chip] = coupled + a1[step]
        wait_a2 = offer(a2.at[step], chip, chips)

        rv, rp = section_of(total, 2), section_of(total, 3)
        if step:
            block = block - dot(pv_spread[:ROWS, :ROWS], basis, precision=HIGHEST)
            crossed = dot(rv, pv_spread, nt=True, precision=HIGHEST)
            crossed_t = dot(pv, spread(rv, mask), nt=True, precision=HIGHEST)
            inner = dot(pv, spread(own_energy, mask), precision=HIGHEST)
            rp = rp - crossed - crossed_t + dot(inner, pv_spread, nt=True, precision=HIGHEST)
        basis = dot(inverse_spread[:ROWS, :ROWS], block, precision=HIGHEST)
        half = dot(inverse, spread(rp, mask), precision=HIGHEST)
        own_energy = dot(half, inverse_spread, nt=True, precision=HIGHEST)

        await_bytes(r2_size, recv, r2_index)
        r3[step, t] = add_up(r2.at[step], CHIPS).astype(BF16)
        wait_r3 = offer(r3.at[step], t, tiles)
        wait_a2()
        a3[step, t] = add_up(a2.at[step], CHIPS)
        wait_a3 = offer(a3.at[step], t, tiles)
        wait_r3()
        sigma = energy * basis + by_k_point(add_up(r3.at[step], TILE), False)
        wait_a3()
        ray_t = fold(add_up(a3.at[step], TILE)) * (1.0 / count) + own_energy
        residual = sigma - dot(spread(ray_t, mask)[:ROWS, :ROWS], basis, precision=HIGHEST)
        block = residual / energy
        sums = grams(
            jnp.concatenate([block, residual], 0), jnp.concatenate([basis, block], 0)
        )
        eye = (iota((NV, SPAN), 0) == iota((NV, SPAN), 1)).astype(F32)
        first = jnp.where(iota((NV, SPAN), 1) < NV, ray_t, 0.0)
        ray_ref[step] = dot(eye, first, nt=True, precision=HIGHEST)

    group, sub = iota((NV, SPAN), 1) // NV, iota((NV, SPAN), 0)
    row = jnp.where(group == sub, section_of(sums, 0), 0.0)
    row = jnp.where(group == sub + NV, section_of(sums, 1), row)
    row = jnp.sum(row, axis=0, keepdims=True)
    f1[0] = row
    hand(f1.at[0], f1.at[1])()
    y = y_hi * 2 + y_lo
    slot = (y * 4 + x) * 4 + z
    f2[slot] = row + f1[1]
    index = next(numbers)
    steps = [(a, b, c) for a in range(4) for b in range(4) for c in range(4)]
    steps.sort(key=lambda o: -sum(min(i, 4 - i) for i in o))
    for a, b, c in steps[:-1]:
        to_y = lax.rem(y + a, 4)
        device = (
            (lax.rem(to_y, 2) * 4 + lax.rem(x + b, 4)) * CORES + core,
            lax.div(to_y, 2) * 4 + lax.rem(z + c, 4),
        )
        push(f2.at[slot], f2.at[slot], index, device)
    res_ref[...] = residual
    for ref, sent in used:
        await_bytes(ref, send, sent)
    used = [(f2.at[pl.ds(0, len(steps) - 1)], index)]
    await_bytes(used[0][0], recv, index)
    total = f2[0]
    for i in range(1, len(steps)):
        total = total + f2[i]
    total = jnp.broadcast_to(total, (NV, SPAN))
    pv = fold(jnp.where(group == sub, total, 0.0))
    pp = fold(jnp.where(group == sub + NV, total, 0.0))
    pv_spread = spread(pv, mask)
    gram = pp - dot(pv, pv_spread, nt=True, precision=HIGHEST)
    inverse_spread = spread(factor(gram)[0], mask)
    block = block - dot(pv_spread[:ROWS, :ROWS], basis, precision=HIGHEST)
    basis_ref[...] = dot(inverse_spread[:ROWS, :ROWS], block, precision=HIGHEST)

    for ref, index in used:
        await_bytes(ref, send, index)


def hand_out(ray, basis, residual, ray_out, basis_out, residual_out):
    basis_out[...] = basis[...]
    residual_out[...] = residual[...]
    ray_out[...] = ray[...]


def per_device(coeff, energy, ranks, assign, screen, initial):
    width = initial.shape[2]
    count = initial.shape[0] * GRP * width * TILE
    vmem = pl.BlockSpec(memory_space=pltpu.VMEM)
    hbm = pl.BlockSpec(memory_space=pltpu.HBM)
    ray, basis, residual = pl.pallas_call(
        functools.partial(body, count),
        out_shape=[
            jax.ShapeDtypeStruct((ITERS, NV, NV), F32),
            jax.ShapeDtypeStruct((ROWS, width), F32),
            jax.ShapeDtypeStruct((ROWS, width), F32),
        ],
        in_specs=[hbm] * 6,
        out_specs=[vmem, vmem, vmem],
        scratch_shapes=[
            pltpu.VMEM(coeff.shape, BF16),
            pltpu.VMEM(screen.shape, BF16),
            pltpu.VMEM((ITERS, TILE, NV, SPAN), F32),
            pltpu.VMEM((ITERS, CORES, CHIPS, NV, SPAN), F32),
            pltpu.VMEM((ITERS, CORES, CHIPS, NV, SPAN), F32),
            pltpu.VMEM((ITERS, TILE, ROWS, LEV), F32),
            pltpu.VMEM((ITERS, CORES, CHIPS, ROWS, LEV), BF16),
            pltpu.VMEM((ALL, LEV), F32),
            pltpu.VMEM((ALL, LEV), BF16),
            pltpu.VMEM((ALL // 2, LEV), F32),
            pltpu.VMEM((ALL // 2, LEV), F32),
            pltpu.VMEM((ALL, ALL // 2), BF16),
            pltpu.VMEM((ALL // 2, ALL), BF16),
            pltpu.VMEM((ALL // 2, SPAN), BF16),
            pltpu.VMEM((ALL // 2, LEV), F32),
            pltpu.VMEM((ITERS, ALL // 2, LEV), BF16),
            pltpu.VMEM((ITERS, ALL // 2, LEV), BF16),
            pltpu.VMEM((ITERS, NV, SPAN), F32),
            pltpu.VMEM((ITERS, NV, SPAN), F32),
            pltpu.VMEM((ITERS, CHIPS, ROWS, LEV), BF16),
            pltpu.VMEM((ITERS, CHIPS, ROWS, LEV), BF16),
            pltpu.VMEM((ITERS, CHIPS, NV, SPAN), F32),
            pltpu.VMEM((ITERS, TILE, ROWS, LEV), BF16),
            pltpu.VMEM((ITERS, TILE, NV, SPAN), F32),
            pltpu.VMEM((CORES, 1, SPAN), F32),
            pltpu.VMEM((CHIPS * TILE, 1, SPAN), F32),
            pltpu.SMEM(assign.shape, jnp.int32),
            pltpu.VMEM(ranks.shape, jnp.int32),
            pltpu.VMEM(energy.shape, F32),
            pltpu.VMEM((ROWS, width), F32),
            pltpu.SemaphoreType.DMA((6,)),
            pltpu.SemaphoreType.DMA((SEMS,)),
            pltpu.SemaphoreType.DMA((SEMS,)),
        ],
        compiler_params=pltpu.CompilerParams(
            collective_id=0, has_side_effects=True, vmem_limit_bytes=32 * 2**20
        ),
        name="davidson",
    )(*[pltpu.with_memory_space_constraint(a, pltpu.HBM) for a in (assign, ranks, coeff, screen, energy, initial.reshape(ROWS, width))])
    basis, residual = basis.reshape(initial.shape), residual.reshape(initial.shape)
    results = (ray, basis, residual)
    return tuple(pl.pallas_call(
        hand_out,
        out_shape=[jax.ShapeDtypeStruct(r.shape, r.dtype) for r in results],
        in_specs=[vmem] * 3,
        out_specs=[vmem] * 3,
        compiler_params=pltpu.CompilerParams(vmem_limit_bytes=8 * 2**20),
        name="hand_out",
    )(*results))


def solution(mesh):
    placed = (
        P("grp", None, "tile"),
        P("grp", "tile"),
        P(),
        P(("grp", "tile")),
        P(("grp", "tile"), None, None),
        P("grp", None, "tile"),
    )
    return jax.shard_map(
        per_device,
        mesh=mesh,
        in_specs=placed,
        out_specs=(P(), P("grp", None, "tile"), P("grp", None, "tile")),
        check_vma=False,
    )
```

```python
import functools

import jax
import jax.numpy as jnp
from jax import lax
from jax.experimental import pallas as pl
from jax.experimental.pallas import tpu as pltpu
from jax.sharding import PartitionSpec as P

ITERS = 2
NV = 8
GRP, TILE, CHIPS, CORES = 16, 8, 8, 2
LK = 4
ROWS = LK * NV
ALL = GRP * ROWS
LEV = 256
TASKS = 32
SEMS = 64
SPAN = 128
F32, BF16 = jnp.float32, jnp.bfloat16
HIGHEST = lax.Precision.HIGHEST
MESH = pl.DeviceIdType.MESH
CHIP_STEPS = ((1, 2), (0, 2), (1, 1), (1, 3), (0, 1), (0, 3), (1, 0))
TILE_STEPS = ((1, 2), (1, 1), (1, 3), (1, 0), (0, 2), (0, 1), (0, 3))


def dot(a, b, nt=False, precision=None):
    return lax.dot_general(
        a, b, (((1,), (1 if nt else 0,)), ((), ())),
        precision=precision, preferred_element_type=F32,
    )


def split(a):
    high = a.astype(BF16)
    return high, (a - high.astype(F32)).astype(BF16)


def dot3(a, b, nt=False):
    rows = a.shape[0]
    high, low = split(b)
    both = jnp.concatenate([a, a - a.astype(BF16).astype(F32)], axis=0).astype(BF16)
    first = dot(both, high, nt=nt)
    return first[:rows] + (first[rows:] + dot(both[:rows], low, nt=nt))


def iota(shape, dim):
    return lax.broadcasted_iota(jnp.int32, shape, dim)


def block_mask(rows, cols):
    return (iota((rows, cols), 0) // NV) == (iota((rows, cols), 1) // NV)


def fold(part):
    for step in (8, 16, 32, 64):
        part = part + pltpu.roll(part, step, 1)
    return part


def sum_groups(a):
    total = a[0:NV]
    for i in range(1, a.shape[0] // NV):
        total = total + a[i * NV:(i + 1) * NV]
    return total


def spread(small, mask):
    return jnp.where(mask, jnp.concatenate([small] * (SPAN // NV), axis=0), 0.0)


def factor(gram, ridge=False):
    whole = (NV, SPAN)
    columns = [jnp.broadcast_to(gram[:, m:m + 1], whole) for m in range(NV)]
    e = [[jnp.broadcast_to(columns[m][n:n + 1, :], whole) for m in range(n + 1)] for n in range(NV)]
    if ridge:
        trace = e[0][0]
        for n in range(1, NV):
            trace = trace + e[n][n]
        for n in range(NV):
            e[n][n] = e[n][n] + (trace * 1e-6 + 1e-30)
    unit = [[None] * NV for _ in range(NV)]
    for j in range(NV):
        inverse_pivot = 1.0 / e[j][j]
        for i in range(j + 1, NV):
            unit[i][j] = e[i][j] * inverse_pivot
            for m in range(j + 1, i + 1):
                e[i][m] = e[i][m] - unit[i][j] * e[m][j]
    back = [[None] * NV for _ in range(NV)]
    for j in range(NV):
        for i in range(j + 1, NV):
            value = unit[i][j]
            for q in range(j + 1, i):
                value = value + unit[i][q] * back[q][j]
            back[i][j] = -value
    scale = [lax.rsqrt(e[n][n]) for n in range(NV)]
    root = [e[n][n] * scale[n] for n in range(NV)]
    sub, lane = iota(whole, 0), iota(whole, 1) % NV

    def assemble(entry):
        out = jnp.zeros(whole, F32)
        for i in range(NV):
            row = jnp.zeros(whole, F32)
            for j in range(i + 1):
                row = jnp.where(lane == j, entry(i, j), row)
            out = jnp.where(sub == i, row, out)
        return out

    inverse = assemble(lambda i, j: scale[i] if i == j else scale[i] * back[i][j])
    lower = assemble(lambda i, j: root[i] if i == j else unit[i][j] * root[j])
    return inverse, lower


def body(
    count, assign_hbm, ranks_hbm, coeff_hbm, screen_hbm, energy_hbm, x_hbm,
    ray_ref, basis_ref, res_ref,
    coeff, screen, g1, g2, t2, d1, d2, dens, dens_b, term, before, e8, pick, pick_group, keep,
    r1s, r1, a1s, a1, r2s, r2, a2, r3, a3, f1, f2,
    assign_ref, ranks_ref, energy_ref, x_ref, load_sem, send, recv,
):
    g, t = lax.axis_index("grp"), lax.axis_index("tile")
    core, chip = lax.rem(g, CORES), lax.div(g, CORES)
    y_lo, x = lax.div(chip, 4), lax.rem(chip, 4)
    y_hi, z = lax.div(t, 4), lax.rem(t, 4)
    sibling = (chip * CORES + (1 - core), t)
    to_ids = [lax.rem(y_lo + a, 2) * 4 + lax.rem(x + b, 4) for a, b in CHIP_STEPS]
    from_ids = [lax.rem(y_lo + 2 - a, 2) * 4 + lax.rem(x + 4 - b, 4) for a, b in CHIP_STEPS]
    chips = [(c * CORES + core, t) for c in to_ids]
    tiles = [(g, lax.rem(y_hi + a, 2) * 4 + lax.rem(z + b, 4)) for a, b in TILE_STEPS]

    half_rows = ALL // 2
    barrier = pltpu.get_barrier_semaphore()
    peers = [*tiles, *chips, sibling]
    for peer in peers:
        pl.semaphore_signal(barrier, inc=1, device_id=peer, device_id_type=MESH)
    loads = [
        pltpu.make_async_copy(src, dst, load_sem.at[i])
        for i, (src, dst) in enumerate((
            (x_hbm, x_ref), (energy_hbm, energy_ref), (coeff_hbm, coeff),
            (assign_hbm, assign_ref), (ranks_hbm, ranks_ref), (screen_hbm, screen),
        ))
    ]
    for load in loads:
        load.start()

    used = []
    numbers = iter(range(SEMS))

    def push(src, dst, index, device):
        pltpu.make_async_remote_copy(
            src_ref=src, dst_ref=dst, send_sem=send.at[index], recv_sem=recv.at[index],
            device_id=device, device_id_type=MESH,
        ).start()

    def await_bytes(ref, sems, index):
        pltpu.make_async_copy(ref, ref, sems.at[index]).wait()

    def offer(buf, mine, devices):
        index = next(numbers)
        for device in devices:
            push(buf.at[mine], buf.at[mine], index, device)
        size = buf.at[pl.ds(0, len(devices))]
        used.append((size, index))
        return lambda: await_bytes(size, recv, index)

    def hand(src, dst):
        index = next(numbers)
        push(src, dst, index, sibling)
        used.append((dst, index))
        return lambda: await_bytes(dst, recv, index)

    def add_up(buf, n):
        total = buf[0].astype(F32)
        for i in range(1, n):
            total = total + buf[i].astype(F32)
        return total

    mask = block_mask(SPAN, SPAN)
    mask_gram = ((iota((2 * ROWS, 2 * ROWS), 0) % ROWS) // NV) == (
        (iota((2 * ROWS, 2 * ROWS), 1) % ROWS) // NV
    )
    section = iota((NV, SPAN), 1) // ROWS

    def grams(left, right):
        full = jnp.where(mask_gram, dot3(left, right, nt=True), 0.0)
        return jnp.concatenate([sum_groups(full[:ROWS]), sum_groups(full[ROWS:])], axis=1)

    def store_ray(step):
        eye = (iota((NV, SPAN), 0) == iota((NV, SPAN), 1)).astype(F32)
        first = jnp.where(iota((NV, SPAN), 1) < NV, ray_t, 0.0)
        ray_ref[step] = dot(eye, first, nt=True, precision=HIGHEST)

    def by_k_point(block, nt):
        low = block - block.astype(BF16).astype(F32)
        out = []
        for k in range(LK):
            rows = slice(k * NV, (k + 1) * NV)
            both = jnp.concatenate([block[rows], low[rows]], axis=0).astype(BF16)
            got = dot(both, coeff[k], nt=nt)
            out.append(got[:NV] + got[NV:])
        return jnp.concatenate(out, axis=0)

    def section_of(total, which):
        return fold(jnp.where(section == which, total, 0.0)) * (1.0 / count)

    def place(k):
        return ((k >> 2) & 1) * half_rows + (k >> 3) * ROWS + (k & 3) * NV

    def one_hots():
        for load in loads[3:5]:
            load.wait()
        lane_task = iota((1, half_rows), 1) // NV
        target = jnp.zeros((1, half_rows), jnp.int32)
        pairs = []
        for i in range(TASKS):
            pair = assign_ref[i]
            target = jnp.where(lane_task == i, place(pair >> 6), target)
            pairs.append(jnp.full((NV, SPAN), pair, jnp.int32))
        target = target + iota((1, half_rows), 1) % NV
        e8[...] = (iota((ALL, half_rows), 0) == target).astype(F32).astype(BF16)
        pairs = jnp.concatenate(pairs, axis=0)
        task_row, task_col = pairs >> 6, pairs & 63
        lane = iota((half_rows, SPAN), 1)
        source_row = place(task_col) + iota((half_rows, SPAN), 0) % NV
        for j in range(ALL // SPAN):
            pick[:, j * SPAN:(j + 1) * SPAN] = (
                (lane + j * SPAN == source_row).astype(F32).astype(BF16)
            )
        group_row = (place(task_col) // ROWS) * NV + iota((half_rows, SPAN), 0) % NV
        pick_group[...] = (lane == group_row).astype(F32).astype(BF16)
        k_points = GRP * LK
        chosen = dot((lane[:, :k_points] == task_row[:, :k_points]).astype(F32).astype(BF16),
                     ranks_ref[...].astype(F32).astype(BF16))
        chosen = jnp.where(lane[:, :k_points] == task_col[:, :k_points], chosen, 0.0)
        rank = jnp.sum(chosen, axis=1, keepdims=True)
        keep[...] = (iota((half_rows, LEV), 1).astype(F32) < rank).astype(F32)

    def apply(high, low, rows):
        rows_high, rows_low = split(rows)
        return (
            dot(jnp.concatenate([high, high], axis=1), jnp.concatenate([rows_high, rows_low], axis=0))
            + dot(low, rows_high)
        )

    for load in loads[:2]:
        load.wait()
    energy = jnp.concatenate(
        [jnp.broadcast_to(energy_ref[k:k + 1, :], (NV, energy_ref.shape[1])) for k in range(LK)],
        axis=0,
    )
    block = x_ref[...]
    zeros = jnp.zeros_like(block)
    sums = grams(jnp.concatenate([block, energy * block], 0), jnp.concatenate([zeros, block], 0))
    loads[2].wait()
    payload = by_k_point(block, True)
    pl.semaphore_wait(barrier, len(peers))

    basis = None
    own_energy = None
    residual = None
    mine = pl.ds(pl.multiple_of(core * half_rows, half_rows), half_rows)
    theirs = pl.ds(pl.multiple_of((1 - core) * half_rows, half_rows), half_rows)
    for step in range(ITERS):
        g1[step, t] = sums
        wait_g1 = offer(g1.at[step], t, tiles)
        if step:
            payload = by_k_point(block, True)
        d1[step, t] = payload
        wait_d1 = offer(d1.at[step], t, tiles)
        if step == 0:
            one_hots()
        else:
            store_ray(step - 1)
        wait_g1()
        total = add_up(g1.at[step], TILE)
        g2[step, core, chip] = total
        wait_g2 = offer(g2.at[step, core], chip, chips)
        own_inverse, own_factor = factor(section_of(total, 1), ridge=True)
        t2[step, core, chip] = own_factor
        wait_t2 = offer(t2.at[step, core], chip, chips)
        own_inverse = spread(own_inverse, mask)[:ROWS, :ROWS]
        wait_d1()
        total = add_up(d1.at[step], TILE)
        d2[step, core, chip] = dot3(own_inverse, total).astype(BF16)
        mine_now = d2.at[step, core, chip]
        arrivals = [next(numbers) for _ in chips]
        for index, device in zip(arrivals, chips):
            push(mine_now, mine_now, index, device)
            used.append((mine_now, index))
        pass_on = next(numbers)
        push(mine_now, mine_now, pass_on, sibling)
        wait_g2()
        wait_h2 = hand(g2.at[step, core], g2.at[step, core])
        wait_t2()
        wait_u2 = hand(t2.at[step, core], t2.at[step, core])
        for index, source in reversed(list(zip(arrivals, from_ids))):
            landed = d2.at[step, core, source]
            await_bytes(landed, recv, index)
            push(landed, landed, pass_on, sibling)
        wait_h2()
        wait_u2()
        whole = d2.at[step, 0]
        used.append((whole, pass_on))
        await_bytes(whole, recv, pass_on)
        if step == 0:
            loads[5].wait()
        chosen = dot(pick[...], d2[step].reshape(ALL, LEV)) * keep[...]
        for i in range(TASKS):
            rows = slice(i * NV, (i + 1) * NV)
            term[rows, :] = dot(chosen[rows].astype(BF16), screen[i], nt=True)

        total = jnp.zeros((NV, SPAN), F32)
        for i in range(CHIPS):
            for c in range(CORES):
                total = total + g2[step, c, i]
        pv, pp = section_of(total, 0), section_of(total, 1)
        pv_spread = spread(pv, mask)
        gram = pp
        if step:
            gram = pp - dot3(pv, pv_spread, nt=True)
        inverse, _ = factor(gram)
        inverse_spread = spread(inverse, mask)
        columns = [jnp.broadcast_to(inverse[:, m:m + 1], (NV, SPAN)) for m in range(NV)]
        mixed_t = []
        for j in range(GRP):
            theirs_t = t2[step, j // CHIPS, j % CHIPS]
            mixed = columns[0] * theirs_t[0:1, :]
            for m in range(1, NV):
                mixed = mixed + columns[m] * theirs_t[m:m + 1, :]
            mixed_t.append(mixed)
        group_high, group_low = split(jnp.concatenate(mixed_t, axis=0))
        if step:
            old = dot3(inverse, pv_spread)
            old_high, old_low = split(spread(old, mask))
        terms = []
        for j in range(half_rows // SPAN):
            rows = slice(j * SPAN, (j + 1) * SPAN)
            high = jnp.where(mask, dot(pick_group[rows, :], group_high), 0.0).astype(BF16)
            low = jnp.where(mask, dot(pick_group[rows, :], group_low), 0.0).astype(BF16)
            result = apply(high, low, term[rows, :])
            if step:
                result = result - apply(old_high, old_low, before[rows, :])
            if step + 1 < ITERS:
                before[rows, :] = result
            terms.append(result)
        term_high, term_low = split(jnp.concatenate(terms, axis=0) * keep[...])

        r1s[step] = (dot(e8[theirs, :], term_high) + dot(e8[theirs, :], term_low)).astype(BF16)
        wait_r1 = hand(r1s.at[step], r1.at[step])
        for j in range(ALL // SPAN):
            rows = slice(j * SPAN, (j + 1) * SPAN)
            parts = [mixed_t[j * 4 + i] for i in range(4) for _ in range(LK)]
            high, low = split(jnp.where(mask, jnp.concatenate(parts, axis=0), 0.0))
            landed = d2[step, j // 2, (j % 2) * 4:(j % 2) * 4 + 4].reshape(SPAN, LEV)
            mixed = dot(high, landed) + dot(low, landed)
            if step:
                mixed = mixed - apply(old_high, old_low, dens[rows, :])
            dens_b[rows, :] = mixed.astype(BF16)
            if step + 1 < ITERS:
                dens[rows, :] = mixed
        own = dot(e8[mine, :], term_high) + dot(e8[mine, :], term_low)
        own_b = own.astype(BF16)
        coupled = jnp.zeros((SPAN, SPAN), F32)
        for j in range(half_rows // SPAN):
            rows = slice(j * SPAN, (j + 1) * SPAN)
            coupled = coupled + dot(r1s[step, rows, :], dens_b[theirs, :][rows], nt=True)
            coupled = coupled + dot(own_b[rows], dens_b[mine, :][rows], nt=True)
        coupled = sum_groups(jnp.where(mask, coupled, 0.0))
        a1s[step] = coupled
        wait_a1 = hand(a1s.at[step], a1.at[step])
        wait_r1()
        summed = (own + r1[step].astype(F32)).astype(BF16)
        for i in range(CHIPS):
            r2s[step, i] = summed[i * ROWS:(i + 1) * ROWS]
        r2_index = next(numbers)
        for c, device in zip(to_ids, chips):
            push(r2s.at[step, c], r2.at[step, chip], r2_index, device)
        r2[step, chip] = r2s[step, chip]
        r2_size = r2.at[step, pl.ds(0, CHIPS - 1)]
        used.append((r2_size, r2_index))
        wait_a1()
        a2[step, chip] = coupled + a1[step]
        wait_a2 = offer(a2.at[step], chip, chips)

        rv, rp = section_of(total, 2), section_of(total, 3)
        if step:
            block = block - dot3(pv_spread[:ROWS, :ROWS], basis)
            crossed = dot3(rv, pv_spread, nt=True)
            crossed_t = dot3(pv, spread(rv, mask), nt=True)
            inner = dot3(pv, spread(own_energy, mask))
            rp = rp - crossed - crossed_t + dot3(inner, pv_spread, nt=True)
        basis = dot3(inverse_spread[:ROWS, :ROWS], block)
        half = dot3(inverse, spread(rp, mask))
        own_energy = dot3(half, inverse_spread, nt=True)

        await_bytes(r2_size, recv, r2_index)
        r3[step, t] = add_up(r2.at[step], CHIPS).astype(BF16)
        wait_r3 = offer(r3.at[step], t, tiles)
        wait_a2()
        a3[step, t] = add_up(a2.at[step], CHIPS)
        wait_a3 = offer(a3.at[step], t, tiles)
        wait_r3()
        sigma = energy * basis + by_k_point(add_up(r3.at[step], TILE), False)
        wait_a3()
        ray_t = fold(add_up(a3.at[step], TILE)) * (1.0 / count) + own_energy
        residual = sigma - dot3(spread(ray_t, mask)[:ROWS, :ROWS], basis)
        block = residual / energy
        sums = grams(
            jnp.concatenate([block, residual], 0), jnp.concatenate([basis, block], 0)
        )

    group, sub = iota((NV, SPAN), 1) // NV, iota((NV, SPAN), 0)
    row = jnp.where(group == sub, section_of(sums, 0), 0.0)
    row = jnp.where(group == sub + NV, section_of(sums, 1), row)
    row = jnp.sum(row, axis=0, keepdims=True)
    f1[0] = row
    hand(f1.at[0], f1.at[1])()
    y = y_hi * 2 + y_lo
    slot = (y * 4 + x) * 4 + z
    f2[slot] = row + f1[1]
    index = next(numbers)
    steps = [(a, b, c) for a in range(4) for b in range(4) for c in range(4)]
    steps.sort(key=lambda o: -sum(min(i, 4 - i) for i in o))
    for a, b, c in steps[:-1]:
        to_y = lax.rem(y + a, 4)
        device = (
            (lax.rem(to_y, 2) * 4 + lax.rem(x + b, 4)) * CORES + core,
            lax.div(to_y, 2) * 4 + lax.rem(z + c, 4),
        )
        push(f2.at[slot], f2.at[slot], index, device)
    res_ref[...] = residual
    store_ray(ITERS - 1)
    for ref, sent in used:
        await_bytes(ref, send, sent)
    used = [(f2.at[pl.ds(0, len(steps) - 1)], index)]
    await_bytes(used[0][0], recv, index)
    total = f2[0]
    for i in range(1, len(steps)):
        total = total + f2[i]
    total = jnp.broadcast_to(total, (NV, SPAN))
    pv = fold(jnp.where(group == sub, total, 0.0))
    pp = fold(jnp.where(group == sub + NV, total, 0.0))
    pv_spread = spread(pv, mask)
    gram = pp - dot3(pv, pv_spread, nt=True)
    inverse_spread = spread(factor(gram)[0], mask)
    block = block - dot3(pv_spread[:ROWS, :ROWS], basis)
    basis_ref[...] = dot3(inverse_spread[:ROWS, :ROWS], block)

    for ref, index in used:
        await_bytes(ref, send, index)


def hand_out(ray, basis, residual, ray_out, basis_out, residual_out):
    basis_out[...] = basis[...]
    residual_out[...] = residual[...]
    ray_out[...] = ray[...]


def per_device(coeff, energy, ranks, assign, screen, initial):
    width = initial.shape[2]
    count = initial.shape[0] * GRP * width * TILE
    vmem = pl.BlockSpec(memory_space=pltpu.VMEM)
    hbm = pl.BlockSpec(memory_space=pltpu.HBM)
    ray, basis, residual = pl.pallas_call(
        functools.partial(body, count),
        out_shape=[
            jax.ShapeDtypeStruct((ITERS, NV, NV), F32),
            jax.ShapeDtypeStruct((ROWS, width), F32),
            jax.ShapeDtypeStruct((ROWS, width), F32),
        ],
        in_specs=[hbm] * 6,
        out_specs=[vmem, vmem, vmem],
        scratch_shapes=[
            pltpu.VMEM(coeff.shape, BF16),
            pltpu.VMEM(screen.shape, BF16),
            pltpu.VMEM((ITERS, TILE, NV, SPAN), F32),
            pltpu.VMEM((ITERS, CORES, CHIPS, NV, SPAN), F32),
            pltpu.VMEM((ITERS, CORES, CHIPS, NV, SPAN), F32),
            pltpu.VMEM((ITERS, TILE, ROWS, LEV), F32),
            pltpu.VMEM((ITERS, CORES, CHIPS, ROWS, LEV), BF16),
            pltpu.VMEM((ALL, LEV), F32),
            pltpu.VMEM((ALL, LEV), BF16),
            pltpu.VMEM((ALL // 2, LEV), F32),
            pltpu.VMEM((ALL // 2, LEV), F32),
            pltpu.VMEM((ALL, ALL // 2), BF16),
            pltpu.VMEM((ALL // 2, ALL), BF16),
            pltpu.VMEM((ALL // 2, SPAN), BF16),
            pltpu.VMEM((ALL // 2, LEV), F32),
            pltpu.VMEM((ITERS, ALL // 2, LEV), BF16),
            pltpu.VMEM((ITERS, ALL // 2, LEV), BF16),
            pltpu.VMEM((ITERS, NV, SPAN), F32),
            pltpu.VMEM((ITERS, NV, SPAN), F32),
            pltpu.VMEM((ITERS, CHIPS, ROWS, LEV), BF16),
            pltpu.VMEM((ITERS, CHIPS, ROWS, LEV), BF16),
            pltpu.VMEM((ITERS, CHIPS, NV, SPAN), F32),
            pltpu.VMEM((ITERS, TILE, ROWS, LEV), BF16),
            pltpu.VMEM((ITERS, TILE, NV, SPAN), F32),
            pltpu.VMEM((CORES, 1, SPAN), F32),
            pltpu.VMEM((CHIPS * TILE, 1, SPAN), F32),
            pltpu.SMEM(assign.shape, jnp.int32),
            pltpu.VMEM(ranks.shape, jnp.int32),
            pltpu.VMEM(energy.shape, F32),
            pltpu.VMEM((ROWS, width), F32),
            pltpu.SemaphoreType.DMA((6,)),
            pltpu.SemaphoreType.DMA((SEMS,)),
            pltpu.SemaphoreType.DMA((SEMS,)),
        ],
        compiler_params=pltpu.CompilerParams(
            collective_id=0, has_side_effects=True, vmem_limit_bytes=32 * 2**20
        ),
        name="davidson",
    )(*[pltpu.with_memory_space_constraint(a, pltpu.HBM) for a in (assign, ranks, coeff, screen, energy, initial.reshape(ROWS, width))])
    basis, residual = basis.reshape(initial.shape), residual.reshape(initial.shape)
    results = (ray, basis, residual)
    return tuple(pl.pallas_call(
        hand_out,
        out_shape=[jax.ShapeDtypeStruct(r.shape, r.dtype) for r in results],
        in_specs=[vmem] * 3,
        out_specs=[vmem] * 3,
        compiler_params=pltpu.CompilerParams(vmem_limit_bytes=8 * 2**20),
        name="hand_out",
    )(*results))


def solution(mesh):
    placed = (
        P("grp", None, "tile"),
        P("grp", "tile"),
        P(),
        P(("grp", "tile")),
        P(("grp", "tile"), None, None),
        P("grp", None, "tile"),
    )
    return jax.shard_map(
        per_device,
        mesh=mesh,
        in_specs=placed,
        out_specs=(P(), P("grp", None, "tile"), P("grp", None, "tile")),
        check_vma=False,
    )
```

```python
import functools

import jax
import jax.numpy as jnp
from jax import lax
from jax.experimental import pallas as pl
from jax.experimental.pallas import tpu as pltpu
from jax.sharding import PartitionSpec as P

ITERS = 2
NV = 8
GRP, TILE, CHIPS, CORES = 16, 8, 8, 2
LK = 4
ROWS = LK * NV
ALL = GRP * ROWS
LEV = 256
TASKS = 32
SEMS = 64
SPAN = 128
F32, BF16 = jnp.float32, jnp.bfloat16
HIGHEST = lax.Precision.HIGHEST
MESH = pl.DeviceIdType.MESH
CHIP_STEPS = ((1, 2), (0, 2), (1, 1), (1, 3), (0, 1), (0, 3), (1, 0))
TILE_STEPS = ((1, 2), (1, 1), (1, 3), (1, 0), (0, 2), (0, 1), (0, 3))


def dot(a, b, nt=False, precision=None):
    return lax.dot_general(
        a, b, (((1,), (1 if nt else 0,)), ((), ())),
        precision=precision, preferred_element_type=F32,
    )


def split(a):
    high = a.astype(BF16)
    return high, (a - high.astype(F32)).astype(BF16)


def dot3(a, b, nt=False):
    rows = a.shape[0]
    high, low = split(b)
    both = jnp.concatenate([a, a - a.astype(BF16).astype(F32)], axis=0).astype(BF16)
    first = dot(both, high, nt=nt)
    return first[:rows] + (first[rows:] + dot(both[:rows], low, nt=nt))


def iota(shape, dim):
    return lax.broadcasted_iota(jnp.int32, shape, dim)


def block_mask(rows, cols):
    return (iota((rows, cols), 0) // NV) == (iota((rows, cols), 1) // NV)


def fold(part):
    for step in (8, 16, 32, 64):
        part = part + pltpu.roll(part, step, 1)
    return part


def sum_groups(a):
    total = a[0:NV]
    for i in range(1, a.shape[0] // NV):
        total = total + a[i * NV:(i + 1) * NV]
    return total


def spread(small, mask):
    return jnp.where(mask, jnp.concatenate([small] * (SPAN // NV), axis=0), 0.0)


def factor(gram, ridge=False):
    whole = (NV, SPAN)
    columns = [jnp.broadcast_to(gram[:, m:m + 1], whole) for m in range(NV)]
    e = [[jnp.broadcast_to(columns[m][n:n + 1, :], whole) for m in range(n + 1)] for n in range(NV)]
    if ridge:
        trace = e[0][0]
        for n in range(1, NV):
            trace = trace + e[n][n]
        for n in range(NV):
            e[n][n] = e[n][n] + (trace * 1e-6 + 1e-30)
    unit = [[None] * NV for _ in range(NV)]
    for j in range(NV):
        inverse_pivot = 1.0 / e[j][j]
        for i in range(j + 1, NV):
            unit[i][j] = e[i][j] * inverse_pivot
            for m in range(j + 1, i + 1):
                e[i][m] = e[i][m] - unit[i][j] * e[m][j]
    back = [[None] * NV for _ in range(NV)]
    for j in range(NV):
        for i in range(j + 1, NV):
            value = unit[i][j]
            for q in range(j + 1, i):
                value = value + unit[i][q] * back[q][j]
            back[i][j] = -value
    scale = [lax.rsqrt(e[n][n]) for n in range(NV)]
    root = [e[n][n] * scale[n] for n in range(NV)]
    sub, lane = iota(whole, 0), iota(whole, 1) % NV

    def assemble(entry):
        out = jnp.zeros(whole, F32)
        for i in range(NV):
            row = jnp.zeros(whole, F32)
            for j in range(i + 1):
                row = jnp.where(lane == j, entry(i, j), row)
            out = jnp.where(sub == i, row, out)
        return out

    inverse = assemble(lambda i, j: scale[i] if i == j else scale[i] * back[i][j])
    lower = assemble(lambda i, j: root[i] if i == j else unit[i][j] * root[j])
    return inverse, lower


def body(
    count, assign_hbm, ranks_hbm, coeff_hbm, screen_hbm, energy_hbm, x_hbm,
    ray_ref, basis_ref, res_ref,
    coeff, screen, g1, g2, d1, d2, dens, dens_b, term, before, e8, pick, pick_group, keep,
    r1s, r1, a1s, a1, r2s, r2, a2, r3, a3, f1, f2,
    assign_ref, ranks_ref, energy_ref, x_ref, load_sem, send, recv,
):
    g, t = lax.axis_index("grp"), lax.axis_index("tile")
    core, chip = lax.rem(g, CORES), lax.div(g, CORES)
    y_lo, x = lax.div(chip, 4), lax.rem(chip, 4)
    y_hi, z = lax.div(t, 4), lax.rem(t, 4)
    sibling = (chip * CORES + (1 - core), t)
    to_ids = [lax.rem(y_lo + a, 2) * 4 + lax.rem(x + b, 4) for a, b in CHIP_STEPS]
    from_ids = [lax.rem(y_lo + 2 - a, 2) * 4 + lax.rem(x + 4 - b, 4) for a, b in CHIP_STEPS]
    chips = [(c * CORES + core, t) for c in to_ids]
    tiles = [(g, lax.rem(y_hi + a, 2) * 4 + lax.rem(z + b, 4)) for a, b in TILE_STEPS]

    half_rows = ALL // 2
    barrier = pltpu.get_barrier_semaphore()
    peers = [*tiles, *chips, sibling]
    for peer in peers:
        pl.semaphore_signal(barrier, inc=1, device_id=peer, device_id_type=MESH)
    loads = [
        pltpu.make_async_copy(src, dst, load_sem.at[i])
        for i, (src, dst) in enumerate((
            (x_hbm, x_ref), (energy_hbm, energy_ref), (coeff_hbm, coeff),
            (assign_hbm, assign_ref), (ranks_hbm, ranks_ref), (screen_hbm, screen),
        ))
    ]
    for load in loads:
        load.start()

    used = []
    numbers = iter(range(SEMS))

    def push(src, dst, index, device):
        pltpu.make_async_remote_copy(
            src_ref=src, dst_ref=dst, send_sem=send.at[index], recv_sem=recv.at[index],
            device_id=device, device_id_type=MESH,
        ).start()

    def await_bytes(ref, sems, index):
        pltpu.make_async_copy(ref, ref, sems.at[index]).wait()

    def offer(buf, mine, devices):
        index = next(numbers)
        for device in devices:
            push(buf.at[mine], buf.at[mine], index, device)
        size = buf.at[pl.ds(0, len(devices))]
        used.append((size, index))
        return lambda: await_bytes(size, recv, index)

    def hand(src, dst):
        index = next(numbers)
        push(src, dst, index, sibling)
        used.append((dst, index))
        return lambda: await_bytes(dst, recv, index)

    def add_up(buf, n):
        total = buf[0].astype(F32)
        for i in range(1, n):
            total = total + buf[i].astype(F32)
        return total

    mask = block_mask(SPAN, SPAN)
    mask_gram = ((iota((2 * ROWS, 2 * ROWS), 0) % ROWS) // NV) == (
        (iota((2 * ROWS, 2 * ROWS), 1) % ROWS) // NV
    )
    section = iota((NV, SPAN), 1) // ROWS

    def grams(left, right):
        full = jnp.where(mask_gram, dot3(left, right, nt=True), 0.0)
        return jnp.concatenate([sum_groups(full[:ROWS]), sum_groups(full[ROWS:])], axis=1)

    def store_ray(step):
        eye = (iota((NV, SPAN), 0) == iota((NV, SPAN), 1)).astype(F32)
        first = jnp.where(iota((NV, SPAN), 1) < NV, ray_t, 0.0)
        ray_ref[step] = dot(eye, first, nt=True, precision=HIGHEST)

    def by_k_point(block, nt):
        low = block - block.astype(BF16).astype(F32)
        out = []
        for k in range(LK):
            rows = slice(k * NV, (k + 1) * NV)
            both = jnp.concatenate([block[rows], low[rows]], axis=0).astype(BF16)
            got = dot(both, coeff[k], nt=nt)
            out.append(got[:NV] + got[NV:])
        return jnp.concatenate(out, axis=0)

    def section_of(total, which):
        return fold(jnp.where(section == which, total, 0.0)) * (1.0 / count)

    def place(k):
        return ((k >> 2) & 1) * half_rows + (k >> 3) * ROWS + (k & 3) * NV

    def one_hots():
        for load in loads[3:5]:
            load.wait()
        lane_task = iota((1, half_rows), 1) // NV
        target = jnp.zeros((1, half_rows), jnp.int32)
        pairs = []
        for i in range(TASKS):
            pair = assign_ref[i]
            target = jnp.where(lane_task == i, place(pair >> 6), target)
            pairs.append(jnp.full((NV, SPAN), pair, jnp.int32))
        target = target + iota((1, half_rows), 1) % NV
        e8[...] = (iota((ALL, half_rows), 0) == target).astype(F32).astype(BF16)
        pairs = jnp.concatenate(pairs, axis=0)
        task_row, task_col = pairs >> 6, pairs & 63
        lane = iota((half_rows, SPAN), 1)
        source_row = place(task_col) + iota((half_rows, SPAN), 0) % NV
        for j in range(ALL // SPAN):
            pick[:, j * SPAN:(j + 1) * SPAN] = (
                (lane + j * SPAN == source_row).astype(F32).astype(BF16)
            )
        group_row = (place(task_col) // ROWS) * NV + iota((half_rows, SPAN), 0) % NV
        pick_group[...] = (lane == group_row).astype(F32).astype(BF16)
        k_points = GRP * LK
        chosen = dot((lane[:, :k_points] == task_row[:, :k_points]).astype(F32).astype(BF16),
                     ranks_ref[...].astype(F32).astype(BF16))
        chosen = jnp.where(lane[:, :k_points] == task_col[:, :k_points], chosen, 0.0)
        rank = jnp.sum(chosen, axis=1, keepdims=True)
        keep[...] = (iota((half_rows, LEV), 1).astype(F32) < rank).astype(F32)

    def apply(high, low, rows):
        rows_high, rows_low = split(rows)
        return (
            dot(jnp.concatenate([high, high], axis=1), jnp.concatenate([rows_high, rows_low], axis=0))
            + dot(low, rows_high)
        )

    for load in loads[:2]:
        load.wait()
    energy = jnp.concatenate(
        [jnp.broadcast_to(energy_ref[k:k + 1, :], (NV, energy_ref.shape[1])) for k in range(LK)],
        axis=0,
    )
    block = x_ref[...]
    zeros = jnp.zeros_like(block)
    sums = grams(jnp.concatenate([block, energy * block], 0), jnp.concatenate([zeros, block], 0))
    loads[2].wait()
    payload = by_k_point(block, True)
    pl.semaphore_wait(barrier, len(peers))

    basis = None
    own_energy = None
    residual = None
    mine = pl.ds(pl.multiple_of(core * half_rows, half_rows), half_rows)
    theirs = pl.ds(pl.multiple_of((1 - core) * half_rows, half_rows), half_rows)
    for step in range(ITERS):
        g1[step, t] = sums
        wait_g1 = offer(g1.at[step], t, tiles)
        if step:
            payload = by_k_point(block, True)
        d1[step, t] = payload
        wait_d1 = offer(d1.at[step], t, tiles)
        if step == 0:
            one_hots()
        else:
            store_ray(step - 1)
        wait_g1()
        total = add_up(g1.at[step], TILE)
        g2[step, core, chip, 0:NV] = total
        own_inverse, own_factor = factor(section_of(total, 1), ridge=True)
        g2[step, core, chip, NV:] = own_factor
        wait_g2 = offer(g2.at[step, core], chip, chips)
        own_inverse = spread(own_inverse, mask)[:ROWS, :ROWS]
        wait_d1()
        total = add_up(d1.at[step], TILE)
        d2[step, core, chip] = dot3(own_inverse, total).astype(BF16)
        mine_now = d2.at[step, core, chip]
        arrivals = [next(numbers) for _ in chips]
        for index, device in zip(arrivals, chips):
            push(mine_now, mine_now, index, device)
            used.append((mine_now, index))
        pass_on = next(numbers)
        push(mine_now, mine_now, pass_on, sibling)
        wait_g2()
        wait_h2 = hand(g2.at[step, core], g2.at[step, core])
        for index, source in reversed(list(zip(arrivals, from_ids))):
            landed = d2.at[step, core, source]
            await_bytes(landed, recv, index)
            push(landed, landed, pass_on, sibling)
        wait_h2()
        whole = d2.at[step, 0]
        used.append((whole, pass_on))
        await_bytes(whole, recv, pass_on)
        if step == 0:
            loads[5].wait()
        chosen = dot(pick[...], d2[step].reshape(ALL, LEV)) * keep[...]
        for i in range(TASKS):
            rows = slice(i * NV, (i + 1) * NV)
            term[rows, :] = dot(chosen[rows].astype(BF16), screen[i], nt=True)

        total = jnp.zeros((NV, SPAN), F32)
        for i in range(CHIPS):
            for c in range(CORES):
                total = total + g2[step, c, i, 0:NV]
        pv, pp = section_of(total, 0), section_of(total, 1)
        pv_spread = spread(pv, mask)
        gram = pp
        if step:
            gram = pp - dot3(pv, pv_spread, nt=True)
        inverse, _ = factor(gram)
        inverse_spread = spread(inverse, mask)
        columns = [jnp.broadcast_to(inverse[:, m:m + 1], (NV, SPAN)) for m in range(NV)]
        mixed_t = []
        for j in range(GRP):
            theirs_t = g2[step, j // CHIPS, j % CHIPS, NV:]
            mixed = columns[0] * theirs_t[0:1, :]
            for m in range(1, NV):
                mixed = mixed + columns[m] * theirs_t[m:m + 1, :]
            mixed_t.append(mixed)
        group_high, group_low = split(jnp.concatenate(mixed_t, axis=0))
        if step:
            old = dot3(inverse, pv_spread)
            old_high, old_low = split(spread(old, mask))
        terms = []
        for j in range(half_rows // SPAN):
            rows = slice(j * SPAN, (j + 1) * SPAN)
            high = jnp.where(mask, dot(pick_group[rows, :], group_high), 0.0).astype(BF16)
            low = jnp.where(mask, dot(pick_group[rows, :], group_low), 0.0).astype(BF16)
            result = apply(high, low, term[rows, :])
            if step:
                result = result - apply(old_high, old_low, before[rows, :])
            if step + 1 < ITERS:
                before[rows, :] = result
            terms.append(result)
        term_high, term_low = split(jnp.concatenate(terms, axis=0) * keep[...])

        r1s[step] = (dot(e8[theirs, :], term_high) + dot(e8[theirs, :], term_low)).astype(BF16)
        wait_r1 = hand(r1s.at[step], r1.at[step])
        for j in range(ALL // SPAN):
            rows = slice(j * SPAN, (j + 1) * SPAN)
            parts = [mixed_t[j * 4 + i] for i in range(4) for _ in range(LK)]
            high, low = split(jnp.where(mask, jnp.concatenate(parts, axis=0), 0.0))
            landed = d2[step, j // 2, (j % 2) * 4:(j % 2) * 4 + 4].reshape(SPAN, LEV)
            mixed = dot(high, landed) + dot(low, landed)
            if step:
                mixed = mixed - apply(old_high, old_low, dens[rows, :])
            dens_b[rows, :] = mixed.astype(BF16)
            if step + 1 < ITERS:
                dens[rows, :] = mixed
        own = dot(e8[mine, :], term_high) + dot(e8[mine, :], term_low)
        own_b = own.astype(BF16)
        coupled = jnp.zeros((SPAN, SPAN), F32)
        for j in range(half_rows // SPAN):
            rows = slice(j * SPAN, (j + 1) * SPAN)
            coupled = coupled + dot(r1s[step, rows, :], dens_b[theirs, :][rows], nt=True)
            coupled = coupled + dot(own_b[rows], dens_b[mine, :][rows], nt=True)
        coupled = sum_groups(jnp.where(mask, coupled, 0.0))
        a1s[step] = coupled
        wait_a1 = hand(a1s.at[step], a1.at[step])
        wait_r1()
        summed = (own + r1[step].astype(F32)).astype(BF16)
        for i in range(CHIPS):
            r2s[step, i] = summed[i * ROWS:(i + 1) * ROWS]
        r2_index = next(numbers)
        for c, device in zip(to_ids, chips):
            push(r2s.at[step, c], r2.at[step, chip], r2_index, device)
        r2[step, chip] = r2s[step, chip]
        r2_size = r2.at[step, pl.ds(0, CHIPS - 1)]
        used.append((r2_size, r2_index))
        wait_a1()
        a2[step, chip] = coupled + a1[step]
        wait_a2 = offer(a2.at[step], chip, chips)

        rv, rp = section_of(total, 2), section_of(total, 3)
        if step:
            block = block - dot3(pv_spread[:ROWS, :ROWS], basis)
            crossed = dot3(rv, pv_spread, nt=True)
            crossed_t = dot3(pv, spread(rv, mask), nt=True)
            inner = dot3(pv, spread(own_energy, mask))
            rp = rp - crossed - crossed_t + dot3(inner, pv_spread, nt=True)
        basis = dot3(inverse_spread[:ROWS, :ROWS], block)
        half = dot3(inverse, spread(rp, mask))
        own_energy = dot3(half, inverse_spread, nt=True)

        await_bytes(r2_size, recv, r2_index)
        r3[step, t] = add_up(r2.at[step], CHIPS).astype(BF16)
        wait_r3 = offer(r3.at[step], t, tiles)
        wait_a2()
        a3[step, t] = add_up(a2.at[step], CHIPS)
        wait_a3 = offer(a3.at[step], t, tiles)
        wait_r3()
        sigma = energy * basis + by_k_point(add_up(r3.at[step], TILE), False)
        wait_a3()
        ray_t = fold(add_up(a3.at[step], TILE)) * (1.0 / count) + own_energy
        residual = sigma - dot3(spread(ray_t, mask)[:ROWS, :ROWS], basis)
        block = residual / energy
        sums = grams(
            jnp.concatenate([block, residual], 0), jnp.concatenate([basis, block], 0)
        )

    group, sub = iota((NV, SPAN), 1) // NV, iota((NV, SPAN), 0)
    row = jnp.where(group == sub, section_of(sums, 0), 0.0)
    row = jnp.where(group == sub + NV, section_of(sums, 1), row)
    row = jnp.sum(row, axis=0, keepdims=True)
    f1[0] = row
    hand(f1.at[0], f1.at[1])()
    y = y_hi * 2 + y_lo
    slot = (y * 4 + x) * 4 + z
    f2[slot] = row + f1[1]
    index = next(numbers)
    steps = [(a, b, c) for a in range(4) for b in range(4) for c in range(4)]
    steps.sort(key=lambda o: -sum(min(i, 4 - i) for i in o))
    for a, b, c in steps[:-1]:
        to_y = lax.rem(y + a, 4)
        device = (
            (lax.rem(to_y, 2) * 4 + lax.rem(x + b, 4)) * CORES + core,
            lax.div(to_y, 2) * 4 + lax.rem(z + c, 4),
        )
        push(f2.at[slot], f2.at[slot], index, device)
    res_ref[...] = residual
    store_ray(ITERS - 1)
    for ref, sent in used:
        await_bytes(ref, send, sent)
    used = [(f2.at[pl.ds(0, len(steps) - 1)], index)]
    await_bytes(used[0][0], recv, index)
    totals = [f2[i] for i in range(len(steps))]
    while len(totals) > 1:
        totals = [left + right for left, right in zip(totals[::2], totals[1::2])]
    total = totals[0]
    total = jnp.broadcast_to(total, (NV, SPAN))
    pv = fold(jnp.where(group == sub, total, 0.0))
    pp = fold(jnp.where(group == sub + NV, total, 0.0))
    pv_spread = spread(pv, mask)
    gram = pp - dot3(pv, pv_spread, nt=True)
    inverse_spread = spread(factor(gram)[0], mask)
    block = block - dot3(pv_spread[:ROWS, :ROWS], basis)
    basis_ref[...] = dot3(inverse_spread[:ROWS, :ROWS], block)

    for ref, index in used:
        await_bytes(ref, send, index)


def hand_out(ray, basis, residual, ray_out, basis_out, residual_out):
    basis_out[...] = basis[...]
    residual_out[...] = residual[...]
    ray_out[...] = ray[...]


def per_device(coeff, energy, ranks, assign, screen, initial):
    width = initial.shape[2]
    count = initial.shape[0] * GRP * width * TILE
    vmem = pl.BlockSpec(memory_space=pltpu.VMEM)
    hbm = pl.BlockSpec(memory_space=pltpu.HBM)
    ray, basis, residual = pl.pallas_call(
        functools.partial(body, count),
        out_shape=[
            jax.ShapeDtypeStruct((ITERS, NV, NV), F32),
            jax.ShapeDtypeStruct((ROWS, width), F32),
            jax.ShapeDtypeStruct((ROWS, width), F32),
        ],
        in_specs=[hbm] * 6,
        out_specs=[vmem, vmem, vmem],
        scratch_shapes=[
            pltpu.VMEM(coeff.shape, BF16),
            pltpu.VMEM(screen.shape, BF16),
            pltpu.VMEM((ITERS, TILE, NV, SPAN), F32),
            pltpu.VMEM((ITERS, CORES, CHIPS, 2 * NV, SPAN), F32),
            pltpu.VMEM((ITERS, TILE, ROWS, LEV), F32),
            pltpu.VMEM((ITERS, CORES, CHIPS, ROWS, LEV), BF16),
            pltpu.VMEM((ALL, LEV), F32),
            pltpu.VMEM((ALL, LEV), BF16),
            pltpu.VMEM((ALL // 2, LEV), F32),
            pltpu.VMEM((ALL // 2, LEV), F32),
            pltpu.VMEM((ALL, ALL // 2), BF16),
            pltpu.VMEM((ALL // 2, ALL), BF16),
            pltpu.VMEM((ALL // 2, SPAN), BF16),
            pltpu.VMEM((ALL // 2, LEV), F32),
            pltpu.VMEM((ITERS, ALL // 2, LEV), BF16),
            pltpu.VMEM((ITERS, ALL // 2, LEV), BF16),
            pltpu.VMEM((ITERS, NV, SPAN), F32),
            pltpu.VMEM((ITERS, NV, SPAN), F32),
            pltpu.VMEM((ITERS, CHIPS, ROWS, LEV), BF16),
            pltpu.VMEM((ITERS, CHIPS, ROWS, LEV), BF16),
            pltpu.VMEM((ITERS, CHIPS, NV, SPAN), F32),
            pltpu.VMEM((ITERS, TILE, ROWS, LEV), BF16),
            pltpu.VMEM((ITERS, TILE, NV, SPAN), F32),
            pltpu.VMEM((CORES, 1, SPAN), F32),
            pltpu.VMEM((CHIPS * TILE, 1, SPAN), F32),
            pltpu.SMEM(assign.shape, jnp.int32),
            pltpu.VMEM(ranks.shape, jnp.int32),
            pltpu.VMEM(energy.shape, F32),
            pltpu.VMEM((ROWS, width), F32),
            pltpu.SemaphoreType.DMA((6,)),
            pltpu.SemaphoreType.DMA((SEMS,)),
            pltpu.SemaphoreType.DMA((SEMS,)),
        ],
        compiler_params=pltpu.CompilerParams(
            collective_id=0, has_side_effects=True, vmem_limit_bytes=32 * 2**20
        ),
        name="davidson",
    )(*[pltpu.with_memory_space_constraint(a, pltpu.HBM) for a in (assign, ranks, coeff, screen, energy, initial.reshape(ROWS, width))])
    basis, residual = basis.reshape(initial.shape), residual.reshape(initial.shape)
    results = (ray, basis, residual)
    return tuple(pl.pallas_call(
        hand_out,
        out_shape=[jax.ShapeDtypeStruct(r.shape, r.dtype) for r in results],
        in_specs=[vmem] * 3,
        out_specs=[vmem] * 3,
        compiler_params=pltpu.CompilerParams(vmem_limit_bytes=8 * 2**20),
        name="hand_out",
    )(*results))


def solution(mesh):
    placed = (
        P("grp", None, "tile"),
        P("grp", "tile"),
        P(),
        P(("grp", "tile")),
        P(("grp", "tile"), None, None),
        P("grp", None, "tile"),
    )
    return jax.shard_map(
        per_device,
        mesh=mesh,
        in_specs=placed,
        out_specs=(P(), P("grp", None, "tile"), P("grp", None, "tile")),
        check_vma=False,
    )
```
